256 devices in a mesh: pipe: 8 (over y, core), dp: 16 (over x_lo, z), tensor: 2 (over x_hi).
Axes of the slice: x: 4 (x_hi: 2, x_lo: 2; x = x_hi * 2 + x_lo), y: 4, z: 8, core: 2. Of those that a mesh axis runs over, the one named last changes fastest.
Arguments:
- codes_in: bfloat16 [4, 2048, 512], P(None, 'dp'), may hold values from -6 to 6
- lengths: int32 [4, 32], P(None, 'dp'), may hold values from 1 to 64, as said below
- dec_weight: bfloat16 [8, 512, 8192], P('pipe', 'dp', 'tensor'), may hold values from -0.25 to 0.25
- enc_weight: bfloat16 [8, 512, 8192], P('pipe', 'dp', 'tensor'), may hold values from -0.0625 to 0.0625
- head: bfloat16 [512], replicated, may hold values from -0.25 to 0.25
Outputs:
- code_grads: float32 [8, 4, 2048, 512], P('pipe', None, ('dp', 'tensor'))
- dec_grad: float32 [8, 512, 8192], P('pipe', 'dp', 'tensor')
- enc_grad: float32 [8, 512, 8192], P('pipe', 'dp', 'tensor')
The draws below stay inside these ranges and needn't reach their ends.
Inputs may be any that keep to these rules, and one draw needn't show every extreme that they name: `lengths`: positions from a sequence's length to 63 are padding; some sequence is full and some holds one token.
All inputs are finite; a program needn't handle non-finite values.
Results may differ from the reference program's by a relative error of at most 0.04.
Values may be sent and summed in bfloat16 or wider, within the bound.
No kernel may reach another device: no remote copies, remote signals or barrier semaphores. Data moves between devices by JAX's collectives and lax.ppermute only.
A program may use at most 128 MiB of HBM per device.

```python
import jax
import jax.numpy as jnp
from jax import lax

D = 8192
C = 512
LEN = 64
MICRO = 4
SEQS = 32
ROWS = 2048
N_PIPE = 8
N_DP = 16


def draw_lengths(key, part):
    key = jax.random.fold_in(key, 11)
    counts = jax.random.randint(key, (MICRO, SEQS), 1, LEN + 1)
    counts = counts.at[0, 0].set(LEN).at[0, 1].set(1)
    return counts.astype(jnp.int32)


def block_scale(stream_key, extent, shards, low, high):
    factor_of = 1.0
    for axis_at, blocks in shards:
        steps = jax.random.uniform(jax.random.fold_in(jax.random.fold_in(stream_key, 6), axis_at), (blocks,), jnp.float32, low / len(shards), high / len(shards))
        factor_of = factor_of * jnp.repeat(jnp.exp(steps), extent[axis_at] // blocks).reshape((-1,) + (1,) * (len(extent) - 1 - axis_at))
    return factor_of


def noise(own_key, shape, deviation, most, shards=(), kind=jnp.bfloat16):
    level = block_scale(own_key, shape, shards, -0.22, 0.18) if shards else 1.0
    result = jax.random.normal(own_key, shape, jnp.float32) * deviation * level
    return jnp.minimum(jnp.maximum(result, -most), most).astype(kind)


def setup_inputs(seed: int = 0) -> dict:
    key_of = jax.random.split(jax.random.key(seed), 6)
    codes_in = noise(key_of[0], (MICRO, ROWS, C), 1.0, 6.0, ((1, 16),))
    lengths = draw_lengths(jax.random.fold_in(key_of[5], 71), 0)
    dec_weight = noise(key_of[2], (N_PIPE, C, D), C ** -0.5, 0.25, ((0, 8), (1, 16), (2, 2)))
    enc_weight = noise(key_of[3], (N_PIPE, C, D), D ** -0.5, 0.0625, ((0, 8), (1, 16), (2, 2)))
    head = noise(key_of[4], (C,), C ** -0.5, 0.25)
    return dict(codes_in=codes_in, lengths=lengths, dec_weight=dec_weight, enc_weight=enc_weight, head=head)


eps = 1e-05
loss_scale = 512.0

def code_norm(codes):
    values = codes.astype(jnp.float32)
    scales = lax.rsqrt(lax.optimization_barrier(jnp.mean(values * values, axis=-1, keepdims=True)) + eps)
    return (values, scales, (values * scales).astype(jnp.bfloat16))

def silu_slope(hidden):
    sigmoid = jax.nn.sigmoid(hidden)
    return sigmoid * (1.0 + hidden * (1.0 - sigmoid))

def contract_last(left, right):
    return lax.dot_general(left, right, (((1,), (1,)), ((), ())), preferred_element_type=jnp.float32)

def section_forward(codes, decoder, encoder):
    values, scales, normed = code_norm(codes)
    hidden = jnp.dot(normed, decoder, preferred_element_type=jnp.float32)
    gated = jax.nn.silu(hidden).astype(jnp.bfloat16)
    return (values + contract_last(gated, encoder)).astype(jnp.bfloat16)

def group_partials(left, right):
    left_groups = left.astype(jnp.float32).reshape(MICRO, N_DP, 2 * LEN, C)
    right_groups = right.astype(jnp.float32).reshape(MICRO, N_DP, 2 * LEN, D)
    partials = jnp.einsum('mgtc,mgtd->gcd', left_groups, right_groups)
    rounded = lax.optimization_barrier(partials.astype(jnp.bfloat16))
    return lax.optimization_barrier(jnp.sum(rounded.astype(jnp.float32), axis=0))

def input_grad(grad_out, values, scales, summed):
    inner = lax.optimization_barrier(jnp.mean(summed * values, axis=-1, keepdims=True))
    return grad_out.astype(jnp.float32) + scales * summed - values * (scales * scales * scales) * inner

def section_backward(codes, grad_out, decoder, encoder):
    values, scales, normed = code_norm(codes)
    hidden = jnp.dot(normed, decoder, preferred_element_type=jnp.float32)
    gated = jax.nn.silu(hidden).astype(jnp.bfloat16)
    gated_grad = jnp.dot(grad_out, encoder, preferred_element_type=jnp.float32)
    hidden_grad = (gated_grad * silu_slope(hidden)).astype(jnp.bfloat16)
    normed_grad = contract_last(hidden_grad, decoder)
    grad_in = input_grad(grad_out, values, scales, normed_grad)
    return (grad_in, group_partials(normed, hidden_grad), group_partials(grad_out, gated))

def reward_seed(final_codes, head, lengths):
    micro_count, row_count, width = final_codes.shape
    seq_count = lengths.shape[1]
    seq_len = row_count // seq_count
    scores = jnp.dot(final_codes.reshape(-1, width), head, preferred_element_type=jnp.float32)
    scores = scores.reshape(micro_count, seq_count, seq_len)
    positions = jnp.arange(seq_len, dtype=jnp.int32)
    valid_mask = (positions[None, None, :] < lengths[:, :, None]).astype(jnp.float32)
    counts = lengths.astype(jnp.float32)
    rewards = lax.optimization_barrier(jnp.sum(scores * valid_mask, axis=-1)) / counts
    paired = rewards.reshape(micro_count, seq_count // 2, 2)
    weight = loss_scale * jax.nn.sigmoid(paired[..., 1] - paired[..., 0])
    reward_grad = jnp.stack([-weight, weight], axis=-1).reshape(micro_count, seq_count)
    token_grad = (reward_grad / counts)[:, :, None] * valid_mask
    token_grad = token_grad.reshape(micro_count, row_count)
    return (token_grad[:, :, None] * head.astype(jnp.float32)).astype(jnp.bfloat16)

def reference(codes_in, lengths, dec_weight, enc_weight, head):
    codes = codes_in.reshape(MICRO * ROWS, C)
    section_inputs = []
    for section_index in range(N_PIPE):
        section_inputs.append(codes)
        codes = section_forward(codes, dec_weight[section_index], enc_weight[section_index])
    grad_out = reward_seed(codes.reshape(MICRO, ROWS, C), head, lengths).reshape(MICRO * ROWS, C)
    code_grads = []
    dec_grads = []
    enc_grads = []
    for section_index in range(N_PIPE - 1, -1, -1):
        grad_in, dec_part, enc_part = section_backward(section_inputs[section_index], grad_out, dec_weight[section_index], enc_weight[section_index])
        code_grads.insert(0, grad_in.reshape(MICRO, ROWS, C))
        dec_grads.insert(0, dec_part)
        enc_grads.insert(0, enc_part)
        grad_out = grad_in.astype(jnp.bfloat16)
    return (jnp.stack(code_grads), jnp.stack(dec_grads), jnp.stack(enc_grads))
```

```python
import functools

import jax
import jax.numpy as jnp
from jax import lax
from jax.experimental import pallas as pl
from jax.experimental.pallas import tpu as pltpu
from jax.sharding import PartitionSpec as P

eps = 1e-05
loss_scale = 512.0
f32 = jnp.float32
bf16 = jnp.bfloat16

Z = 8
SUB = 32
WIDTH = 512
SPAN = 2048
COLS = 4096
XPART = 768
ZPART = SPAN - XPART
TILE = 1024
CHUNKS = 2
STAGES = 4


def core_swap(value):
    return lax.ppermute(value, "pipe", [(i, i ^ 1) for i in range(8)])


def y_shift(value, steps):
    return lax.ppermute(
        value, "pipe", [(i, i + 2 * steps) for i in range(8) if 0 <= i + 2 * steps < 8]
    )


def z_shift(value, steps):
    return lax.ppermute(
        value, "dp", [(x * Z + z, x * Z + (z + steps) % Z) for x in range(2) for z in range(Z)]
    )


def swap_a(value):
    return lax.ppermute(value, "dp", [(x * Z + z, (1 - x) * Z + z) for x in range(2) for z in range(Z)])


def swap_b(value):
    pairs = [
        ((x * Z + z) * 2 + t, ((1 - x) * Z + z) * 2 + 1 - t)
        for x in range(2)
        for z in range(Z)
        for t in range(2)
    ]
    return lax.ppermute(value, ("dp", "tensor"), pairs)


def gather_x(block):
    half = block.shape[0] // 2
    a = swap_a(block)
    b = swap_b(block)
    d = jnp.concatenate([swap_a(b[:half]), swap_b(a[half:])], axis=0)
    return {(0, 0): block, (0, 1): a, (1, 1): b, (1, 0): d}


def gather_z(block):
    half = block.shape[0] // 2
    out = {0: block}
    up, down = block, block
    for step in (1, 2, 3):
        up = z_shift(up, 1)
        down = z_shift(down, -1)
        out[Z - step] = up
        out[step] = down
    out[4] = (z_shift(up[:half], 1), z_shift(down[half:], -1))
    return out


def copy_kernel(moves, n_in, *refs):
    sources, target, sems = refs[:n_in], refs[n_in + 1], refs[n_in + 2]
    copies = []
    for k, (which, src, dst) in enumerate(moves):
        copy = pltpu.make_async_copy(sources[which].at[src], target.at[dst], sems.at[k])
        copy.start()
        copies.append(copy)
    for copy in copies:
        copy.wait()


def place(buffer, pieces, moves):
    n_in = len(pieces)
    return pl.pallas_call(
        functools.partial(copy_kernel, moves, n_in),
        out_shape=jax.ShapeDtypeStruct(buffer.shape, buffer.dtype),
        in_specs=[pl.BlockSpec(memory_space=pl.ANY)] * (n_in + 1),
        out_specs=pl.BlockSpec(memory_space=pl.ANY),
        scratch_shapes=[pltpu.SemaphoreType.DMA((len(moves),))],
        input_output_aliases={n_in: 0},
    )(*pieces, buffer)


def spot(xr, dz, tr, low, high):
    row = xr * Z * SUB + dz * SUB
    return (slice(None), slice(None), slice(row, row + SUB), slice(tr * SPAN + low, tr * SPAN + high))


def gather_weights(dec_weight, enc_weight, core):
    own = jnp.stack([dec_weight[0], enc_weight[0]])
    mine = lax.dynamic_slice_in_dim(own, core * SPAN, SPAN, 2)
    other = core_swap(lax.dynamic_slice_in_dim(own, (1 - core) * SPAN, SPAN, 2))
    first = core == 0
    block = jnp.stack([jnp.where(first, mine, other), jnp.where(first, other, mine)])
    part_x, part_z = block[..., :XPART], block[..., XPART:]

    part_x = gather_x(part_x)
    stacked = jnp.stack(
        [
            jnp.stack([part_x[0, 0], part_x[0, 1]]),
            jnp.stack([part_x[1, 0], part_x[1, 1]]),
        ]
    )
    rings = gather_z(stacked)
    flat = gather_z(part_z)
    flat[4] = jnp.concatenate([flat[4][0], flat[4][1]], axis=0)

    buffer = jnp.zeros((2, 2, WIDTH, COLS), bf16)
    groups = ((7, 0, 1, 2), (3, 4, 5, 6))
    pieces, moves = [], []
    for group in groups:
        wide = gather_x(jnp.stack([flat[dz] for dz in group]))
        for (tr, xr), piece in wide.items():
            for k, dz in enumerate(group):
                moves.append((len(pieces), (k,), spot(xr, dz, tr, XPART, SPAN)))
            pieces.append(piece)
    for dz in range(Z):
        for tr in range(2):
            for xr in range(2):
                if dz == 4:
                    moves.append((len(pieces) + tr, (0, xr), spot(xr, dz, tr, 0, XPART)))
                else:
                    moves.append((len(pieces), (tr, xr), spot(xr, dz, tr, 0, XPART)))
        if dz == 4:
            pieces += [rings[dz][0], rings[dz][1]]
        else:
            pieces.append(rings[dz])
    return place(buffer, pieces, moves)


def add(*terms):
    return functools.reduce(lambda a, b: a + b, [t.astype(f32) for t in terms])


def reduce_x(parts):
    far = parts[1, 0]
    half = far.shape[0] // 2
    from_a = swap_a(far[:half])
    from_b = swap_b(far[half:])
    to_b = jnp.concatenate(
        [add(parts[1, 1][:half], from_a).astype(bf16), parts[1, 1][half:]], axis=0
    )
    to_a = jnp.concatenate(
        [parts[0, 1][:half], add(parts[0, 1][half:], from_b).astype(bf16)], axis=0
    )
    return add(parts[0, 0], swap_a(to_a), swap_b(to_b))


def reduce_z(parts):
    far = parts[4]
    half = far.shape[0] // 2
    up = z_shift(far[:half], 1)
    down = z_shift(far[half:], -1)
    up = jnp.concatenate([add(parts[3][:half], up).astype(bf16), parts[3][half:]], axis=0)
    down = jnp.concatenate([parts[5][:half], add(parts[5][half:], down).astype(bf16)], axis=0)
    up = z_shift(up, 1)
    down = z_shift(down, -1)
    for step in (2, 1):
        up = z_shift(add(parts[step], up).astype(bf16), 1)
        down = z_shift(add(parts[Z - step], down).astype(bf16), -1)
    return add(parts[0], up, down)


def norm_of(codes):
    values = codes.astype(f32)
    scales = lax.rsqrt(jnp.mean(values * values, axis=-1, keepdims=True) + eps)
    return values, scales


def grad_through_norm(grad_out, codes, left, right):
    values, scales = norm_of(codes)
    summed = left.astype(f32) + right.astype(f32)
    inner = jnp.mean(summed * values, axis=-1, keepdims=True)
    return (
        grad_out.astype(f32) + scales * summed - values * (scales * scales * scales) * inner
    )


def dot_rows(left, right):
    return lax.dot_general(left, right, (((1,), (0,)), ((), ())), preferred_element_type=f32)


def dot_last(left, right):
    return lax.dot_general(left, right, (((1,), (1,)), ((), ())), preferred_element_type=f32)


def dot_first(left, right):
    return lax.dot_general(left, right, (((0,), (0,)), ((), ())), preferred_element_type=f32)


def forward_kernel(n_terms, keep, *refs):
    terms, (dec_ref, enc_ref) = refs[:n_terms], refs[n_terms : n_terms + 2]
    outs = refs[n_terms + 2 :]
    code_ref, part_ref = outs[:2]
    normed_ref, total_ref = outs[-2:]
    step = pl.program_id(0)

    @pl.when(step == 0)
    def _():
        codes = terms[1][...].astype(f32)
        if n_terms == 3:
            codes = codes + terms[2][...].astype(f32)
        codes = (terms[0][...].astype(f32) + codes).astype(bf16)
        code_ref[...] = codes
        values, scales = norm_of(codes)
        normed_ref[...] = (values * scales).astype(bf16)
        total_ref[...] = jnp.zeros_like(total_ref)

    half = 0.5 * dot_rows(normed_ref[...], dec_ref[0, 0])
    bend = jnp.tanh(half)
    gated = (half + half * bend).astype(bf16)
    if keep:
        gated_ref, slope_ref = outs[2:4]
        gated_ref[...] = gated
        slope_ref[...] = (0.5 * (1.0 + bend) * (1.0 + half * (1.0 - bend))).astype(bf16)
    total_ref[...] += dot_last(gated, enc_ref[0, 0])

    @pl.when(step == pl.num_programs(0) - 1)
    def _():
        part_ref[...] = total_ref[...].astype(bf16)


def weight_specs(section):
    return [
        pl.BlockSpec((1, 1, WIDTH, TILE), lambda i: (section, 0, 0, i)),
        pl.BlockSpec((1, 1, WIDTH, TILE), lambda i: (section, 1, 0, i)),
    ]


def section_cost(rows):
    return pl.CostEstimate(
        flops=4 * rows * WIDTH * COLS,
        bytes_accessed=4 * WIDTH * COLS + 8 * rows * WIDTH,
        transcendentals=rows * COLS,
    )


def section_forward(terms, weights, section, keep):
    rows = terms[0].shape[0]
    narrow = pl.BlockSpec((rows, WIDTH), lambda i: (0, 0))
    wide = pl.BlockSpec((rows, TILE), lambda i: (0, i))
    out_shape = [jax.ShapeDtypeStruct((rows, WIDTH), bf16)] * 2
    out_specs = [narrow, narrow]
    if keep:
        out_shape += [jax.ShapeDtypeStruct((rows, COLS), bf16)] * 2
        out_specs += [wide, wide]
    return pl.pallas_call(
        functools.partial(forward_kernel, len(terms), keep),
        grid=(COLS // TILE,),
        in_specs=[narrow] * len(terms) + weight_specs(section),
        out_specs=out_specs,
        out_shape=out_shape,
        scratch_shapes=[pltpu.VMEM((rows, WIDTH), bf16), pltpu.VMEM((rows, WIDTH), f32)],
        compiler_params=pltpu.CompilerParams(vmem_limit_bytes=24 * 1024 * 1024),
        cost_estimate=section_cost(rows),
    )(*terms, weights, weights)


def backward_kernel(n_terms, keep, *refs):
    terms, (slope_ref, dec_ref, enc_ref) = refs[:n_terms], refs[n_terms : n_terms + 3]
    outs = refs[n_terms + 3 :]
    grad_ref, part_ref = outs[:2]
    total_ref = outs[-1]
    step = pl.program_id(0)

    @pl.when(step == 0)
    def _():
        if n_terms == 2:
            grad = terms[0][...].astype(f32) + terms[1][...].astype(f32)
        else:
            grad = grad_through_norm(*[t[...] for t in terms])
        grad_ref[...] = grad.astype(bf16)
        total_ref[...] = jnp.zeros_like(total_ref)

    gated_grad = dot_rows(grad_ref[...], enc_ref[0, 0])
    hidden_grad = (gated_grad * slope_ref[...].astype(f32)).astype(bf16)
    if keep:
        outs[2][...] = hidden_grad
    total_ref[...] += dot_last(hidden_grad, dec_ref[0, 0])

    @pl.when(step == pl.num_programs(0) - 1)
    def _():
        part_ref[...] = total_ref[...].astype(bf16)


def section_backward(terms, slope, weights, section, keep):
    rows = terms[0].shape[0]
    narrow = pl.BlockSpec((rows, WIDTH), lambda i: (0, 0))
    wide = pl.BlockSpec((rows, TILE), lambda i: (0, i))
    out_shape = [jax.ShapeDtypeStruct((rows, WIDTH), bf16)] * 2
    out_specs = [narrow, narrow]
    if keep:
        out_shape += [jax.ShapeDtypeStruct((rows, COLS), bf16)]
        out_specs += [wide]
    return pl.pallas_call(
        functools.partial(backward_kernel, len(terms), keep),
        grid=(COLS // TILE,),
        in_specs=[narrow] * len(terms) + [wide] + weight_specs(section),
        out_specs=out_specs,
        out_shape=out_shape,
        scratch_shapes=[pltpu.VMEM((rows, WIDTH), f32)],
        compiler_params=pltpu.CompilerParams(vmem_limit_bytes=24 * 1024 * 1024),
        cost_estimate=section_cost(rows),
    )(*terms, slope, weights, weights)


def norm_grad_kernel(grad_ref, code_ref, left_ref, right_ref, out_ref):
    out_ref[...] = grad_through_norm(
        grad_ref[...], code_ref[...], left_ref[...], right_ref[...]
    ).astype(out_ref.dtype)


def norm_grad(grad, codes, left, right, dtype):
    return pl.pallas_call(
        norm_grad_kernel, out_shape=jax.ShapeDtypeStruct(grad.shape, dtype)
    )(grad, codes, left, right)


def seed_kernel(flag_ref, lengths_ref, code_ref, left_ref, right_ref, head_ref, out_ref):
    codes = (
        code_ref[...].astype(f32) + (left_ref[...].astype(f32) + right_ref[...].astype(f32))
    ).astype(bf16)
    head = head_ref[...].astype(f32)
    scores = jnp.sum(codes.astype(f32) * head, axis=-1, keepdims=True)
    rows = scores.shape[0]
    seq_len = rows // 2
    position = lax.broadcasted_iota(jnp.int32, (rows, 1), 0)
    chosen_length, other_length = lengths_ref[0], lengths_ref[1]
    chosen = jnp.where(position < seq_len, 1.0, 0.0)
    limit = jnp.where(position < seq_len, chosen_length, other_length + seq_len)
    valid = jnp.where(position < limit, 1.0, 0.0)
    chosen_count = jnp.full((1, 1), chosen_length, jnp.int32).astype(f32)
    other_count = jnp.full((1, 1), other_length, jnp.int32).astype(f32)
    chosen_sum = jnp.sum(scores * valid * chosen, axis=0, keepdims=True)
    other_sum = jnp.sum(scores * valid * (1.0 - chosen), axis=0, keepdims=True)
    gap = other_sum / other_count - chosen_sum / chosen_count
    weight = loss_scale * jax.nn.sigmoid(gap)
    token = (1.0 - chosen) * (weight / other_count) - chosen * (weight / chosen_count)
    token = token * valid * jnp.full((1, 1), flag_ref[0], jnp.int32).astype(f32)
    out_ref[...] = (token * head).astype(bf16)


def reward_seed(flag, lengths, codes, left, right, head):
    vmem = pl.BlockSpec(memory_space=pltpu.VMEM)
    smem = pl.BlockSpec(memory_space=pltpu.SMEM)
    return pl.pallas_call(
        seed_kernel,
        in_specs=[smem, smem, vmem, vmem, vmem, vmem],
        out_specs=vmem,
        out_shape=jax.ShapeDtypeStruct(codes.shape, bf16),
    )(flag, lengths, codes, left, right, head)


def weight_grad_kernel(*refs):
    grads, codes = refs[0:CHUNKS], refs[CHUNKS : 2 * CHUNKS]
    gated, hidden = refs[2 * CHUNKS : 3 * CHUNKS], refs[3 * CHUNKS : 4 * CHUNKS]
    x_ref, z_ref = refs[4 * CHUNKS :]

    def joined(group):
        return jnp.concatenate([ref[0] for ref in group], axis=0)

    values, scales = norm_of(joined(codes))
    normed = (values * scales).astype(bf16)
    for mat, (left, group) in enumerate(((normed, hidden), (joined(grads), gated))):
        for low, high, is_x in ((0, XPART, True), (XPART, SPAN, False)):
            right = jnp.concatenate([ref[0, :, low:high] for ref in group], axis=0)
            result = dot_first(left, right).astype(bf16)
            for xr in range(2):
                for dz in range(Z):
                    row = (xr * Z + dz) * SUB
                    piece = result[row : row + SUB]
                    if is_x:
                        x_ref[dz, 0, xr, 0, mat] = piece
                    else:
                        z_ref[0, xr, dz, 0, mat] = piece


def weight_grads(grads, codes, gated, hidden):
    rows = grads[0].shape[1]
    narrow = pl.BlockSpec((1, rows, WIDTH), lambda s, t: (s, 0, 0))
    wide = pl.BlockSpec((1, rows, SPAN), lambda s, t: (s, 0, t))
    return pl.pallas_call(
        weight_grad_kernel,
        grid=(2, 2),
        in_specs=[narrow] * (2 * CHUNKS) + [wide] * (2 * CHUNKS),
        out_specs=[
            pl.BlockSpec((Z, 1, 2, 1, 2, SUB, XPART), lambda s, t: (0, t, 0, s, 0, 0, 0)),
            pl.BlockSpec((1, 2, Z, 1, 2, SUB, ZPART), lambda s, t: (t, 0, 0, s, 0, 0, 0)),
        ],
        out_shape=[
            jax.ShapeDtypeStruct((Z, 2, 2, 2, 2, SUB, XPART), bf16),
            jax.ShapeDtypeStruct((2, 2, Z, 2, 2, SUB, ZPART), bf16),
        ],
        compiler_params=pltpu.CompilerParams(vmem_limit_bytes=40 * 1024 * 1024),
    )(*grads, *codes, *gated, *hidden)


def to_local(value, pair, z_index):
    lead = value.shape[:-1]
    value = value.reshape(lead + (2, Z, SUB))
    axis = len(lead)
    value = jnp.where(pair == 0, value, jnp.flip(value, axis))
    doubled = jnp.concatenate([value, value], axis=axis + 1)
    return lax.dynamic_slice_in_dim(doubled, z_index, Z, axis + 1).reshape(lead + (WIDTH,))


def to_global(value, pair, z_index):
    return to_local(value, pair, (Z - z_index) % Z)


def on_device(codes_in, lengths, dec_weight, enc_weight, head):
    pipe = lax.axis_index("pipe")
    core, stage = pipe % 2, pipe // 2
    tensor = lax.axis_index("tensor")
    dp = lax.axis_index("dp")
    pair, z_index = dp // Z, dp % Z

    weights = gather_weights(dec_weight, enc_weight, core)

    codes_in = lax.dynamic_slice_in_dim(codes_in, tensor * CHUNKS, CHUNKS, 0)
    lengths = lax.dynamic_slice_in_dim(lengths, tensor * CHUNKS, CHUNKS, 0)
    codes_in = to_local(codes_in, pair, z_index)
    codes_in = jnp.where(stage == 0, codes_in, jnp.zeros_like(codes_in))
    head = to_local(head[None], pair, z_index)
    is_last = (stage == STAGES - 1).astype(jnp.int32)[None]

    rows = codes_in.shape[1]
    blank = jnp.zeros((rows, WIDTH), bf16)
    chunks = range(CHUNKS)
    received = [blank] * CHUNKS
    codes = [[None, None] for _ in chunks]
    gated = [[None, None] for _ in chunks]
    slope = [[None, None] for _ in chunks]
    seeds = [None] * CHUNKS
    for step in range(STAGES):
        keep = step == STAGES - 1
        for m in chunks:
            first = section_forward([received[m], codes_in[m]], weights, 0, keep)
            second = section_forward([first[0], first[1], core_swap(first[1])], weights, 1, keep)
            across = core_swap(second[1])
            if keep:
                codes[m] = [first[0], second[0]]
                gated[m] = [first[2], second[2]]
                slope[m] = [first[3], second[3]]
                seeds[m] = reward_seed(is_last, lengths[m], second[0], second[1], across, head)
            else:
                received[m] = y_shift(add(second[0], add(second[1], across)).astype(bf16), 1)

    received = [blank] * CHUNKS
    grads = [[None, None] for _ in chunks]
    hidden = [[None, None] for _ in chunks]
    parts = [[None, None] for _ in chunks]
    for step in range(STAGES):
        keep = step == STAGES - 1
        for m in chunks:
            second = section_backward([received[m], seeds[m]], slope[m][1], weights, 1, keep)
            second_across = core_swap(second[1])
            first = section_backward(
                [second[0], codes[m][1], second[1], second_across], slope[m][0], weights, 0, keep
            )
            first_across = core_swap(first[1])
            if keep:
                grads[m] = [first[0], second[0]]
                hidden[m] = [first[2], second[2]]
                parts[m] = [(first[1], first_across), (second[1], second_across)]
            else:
                received[m] = y_shift(
                    norm_grad(first[0], codes[m][0], first[1], first_across, bf16), -1
                )

    by_x, by_z = weight_grads(
        [jnp.stack(grads[m]) for m in chunks],
        [jnp.stack(codes[m]) for m in chunks],
        [jnp.stack(gated[m]) for m in chunks],
        [jnp.stack(hidden[m]) for m in chunks],
    )
    summed_x = reduce_z([by_x[dz] for dz in range(Z)]).astype(bf16)
    summed_x = reduce_x({(tr, xr): summed_x[tr, xr] for tr in range(2) for xr in range(2)})
    summed_z = reduce_x({(tr, xr): by_z[tr, xr] for tr in range(2) for xr in range(2)})
    summed_z = reduce_z([summed_z[dz].astype(bf16) for dz in range(Z)])
    summed = jnp.concatenate([summed_x, summed_z], axis=-1)
    mine = lax.dynamic_index_in_dim(summed, core, 0, keepdims=False)
    other = core_swap(lax.dynamic_index_in_dim(summed, 1 - core, 0, keepdims=False))
    full = jnp.where(
        core == 0,
        jnp.concatenate([mine, other], axis=-1),
        jnp.concatenate([other, mine], axis=-1),
    )

    def pick(pairs):
        return jnp.where(core == 0, pairs[0], pairs[1])

    code_grads = []
    for m in chunks:
        code_grads.append(
            norm_grad(
                pick(grads[m]),
                pick(codes[m]),
                pick([parts[m][0][0], parts[m][1][0]]),
                pick([parts[m][0][1], parts[m][1][1]]),
                f32,
            )
        )
    code_grads = to_global(jnp.stack(code_grads), pair, z_index)
    share = rows // 2
    kept = lax.dynamic_slice_in_dim(code_grads, tensor * share, share, 1)
    sent = lax.dynamic_slice_in_dim(code_grads, (1 - tensor) * share, share, 1)
    got = lax.ppermute(sent, "tensor", [(0, 1), (1, 0)])
    code_out = jnp.where(
        tensor == 0, jnp.concatenate([kept, got], axis=0), jnp.concatenate([got, kept], axis=0)
    )
    return (code_out[None], full[0][None], full[1][None])


def solution(mesh):
    in_specs = (
        P(None, "dp", None),
        P(None, "dp"),
        P("pipe", "dp", "tensor"),
        P("pipe", "dp", "tensor"),
        P(),
    )
    out_specs = (
        P("pipe", None, ("dp", "tensor"), None),
        P("pipe", "dp", "tensor"),
        P("pipe", "dp", "tensor"),
    )
    return jax.shard_map(
        on_device, mesh=mesh, in_specs=in_specs, out_specs=out_specs, check_vma=False
    )
```

```python
import functools

import jax
import jax.numpy as jnp
from jax import lax
from jax.experimental import pallas as pl
from jax.experimental.pallas import tpu as pltpu
from jax.sharding import PartitionSpec as P

eps = 1e-05
loss_scale = 512.0
f32 = jnp.float32
bf16 = jnp.bfloat16

Z = 8
SUB = 32
WIDTH = 512
SPAN = 2048
COLS = 4096
XPART = 896
ZPART = SPAN - XPART
TILE = 1024
NEAR = (0, 1, 2, 6, 7)
FAR = (3, 4, 5)
MIB = 1024 * 1024
CHUNKS = 2
STAGES = 4


def core_swap(value):
    return lax.ppermute(value, "pipe", [(i, i ^ 1) for i in range(8)])


def y_shift(value, steps):
    return lax.ppermute(
        value, "pipe", [(i, i + 2 * steps) for i in range(8) if 0 <= i + 2 * steps < 8]
    )


def z_shift(value, steps):
    return lax.ppermute(
        value, "dp", [(x * Z + z, x * Z + (z + steps) % Z) for x in range(2) for z in range(Z)]
    )


def swap_a(value):
    return lax.ppermute(value, "dp", [(x * Z + z, (1 - x) * Z + z) for x in range(2) for z in range(Z)])


def swap_b(value):
    pairs = [
        ((x * Z + z) * 2 + t, ((1 - x) * Z + z) * 2 + 1 - t)
        for x in range(2)
        for z in range(Z)
        for t in range(2)
    ]
    return lax.ppermute(value, ("dp", "tensor"), pairs)


def fenced(*values):
    return lax.optimization_barrier(values)


def copy_kernel(moves, n_in, *refs):
    sources, targets, sems = refs[:n_in], refs[n_in : n_in + 2], refs[n_in + 2]
    copies = []
    for k, (which, src, section, dst) in enumerate(moves):
        copy = pltpu.make_async_copy(
            sources[which].at[src], targets[section].at[dst], sems.at[k]
        )
        copy.start()
        copies.append(copy)
    for copy in copies:
        copy.wait()


def place(pieces, moves):
    vmem = pl.BlockSpec(memory_space=pltpu.VMEM)
    return pl.pallas_call(
        functools.partial(copy_kernel, moves, len(pieces)),
        out_shape=[jax.ShapeDtypeStruct((2, WIDTH, COLS), bf16)] * 2,
        in_specs=[pl.BlockSpec(memory_space=pl.ANY)] * len(pieces),
        out_specs=[vmem, vmem],
        scratch_shapes=[pltpu.SemaphoreType.DMA((len(moves),))],
        compiler_params=pltpu.CompilerParams(vmem_limit_bytes=24 * MIB),
    )(*pieces)


def spot(xr, dz, tr, low, high):
    row = (xr * Z + dz) * SUB
    return (slice(None), slice(row, row + SUB), slice(tr * SPAN + low, tr * SPAN + high))


def gather_weights(dec_weight, enc_weight, core):
    own = jnp.stack([dec_weight[0], enc_weight[0]])
    mine = lax.dynamic_slice_in_dim(own, core * SPAN, SPAN, 2)
    other = core_swap(lax.dynamic_slice_in_dim(own, (1 - core) * SPAN, SPAN, 2))
    first = core == 0
    block = jnp.stack([jnp.where(first, mine, other), jnp.where(first, other, mine)])
    part_x, part_z = block[..., :XPART], block[..., XPART:]

    a, b, u1, d1 = fenced(
        swap_a(part_x), swap_b(part_x), z_shift(part_z, 1), z_shift(part_z, -1)
    )
    da, db, u2, d2 = fenced(swap_a(b[:1]), swap_b(a[1:]), z_shift(u1, 1), z_shift(d1, -1))
    ring = jnp.stack(
        [jnp.stack([part_x, a]), jnp.stack([jnp.concatenate([da, db], axis=0), b])]
    )
    near = jnp.stack([part_z, d1, d2, u2, u1])
    near_a, near_b, w1, v1, u3, d3 = fenced(
        swap_a(near),
        swap_b(near),
        z_shift(ring, 1),
        z_shift(ring, -1),
        z_shift(u2, 1),
        z_shift(d2, -1),
    )
    near_da, near_db, w2, v2, u4, d4 = fenced(
        swap_a(near_b[:, :1]),
        swap_b(near_a[:, 1:]),
        z_shift(w1, 1),
        z_shift(v1, -1),
        z_shift(u3[:1], 1),
        z_shift(d3[1:], -1),
    )
    far = jnp.stack([d3, jnp.concatenate([u4, d4], axis=0), u3])
    far_a, far_b, w3, v3 = fenced(
        swap_a(far), swap_b(far), z_shift(w2, 1), z_shift(v2, -1)
    )
    far_da, far_db, w4, v4 = (
        swap_a(far_b[:, :1]),
        swap_b(far_a[:, 1:]),
        z_shift(w3[:1], 1),
        z_shift(v3[1:], -1),
    )

    pieces, moves = [], []
    for group, own_part, to_a, to_b, half_a, half_b in (
        (NEAR, near, near_a, near_b, near_da, near_db),
        (FAR, far, far_a, far_b, far_da, far_db),
    ):
        for k, dz in enumerate(group):
            for section in range(2):
                for n, (tr, xr) in enumerate(((0, 0), (0, 1), (1, 1))):
                    moves.append(
                        (len(pieces) + n, (k, section), section, spot(xr, dz, tr, XPART, SPAN))
                    )
                moves.append(
                    (len(pieces) + 3 + section, (k, 0), section, spot(0, dz, 1, XPART, SPAN))
                )
        pieces += [own_part, to_a, to_b, half_a, half_b]
    rings = {0: ring, 1: v1, 2: v2, 3: v3, 5: w3, 6: w2, 7: w1}
    for dz in range(Z):
        for section in range(2):
            for tr in range(2):
                for xr in range(2):
                    which, index = (len(pieces) + tr, 0) if dz == 4 else (len(pieces), tr)
                    moves.append(
                        (which, (index, xr, section), section, spot(xr, dz, tr, 0, XPART))
                    )
        pieces += [w4, v4] if dz == 4 else [rings[dz]]
    return place(pieces, moves)


def add(*terms):
    return functools.reduce(lambda a, b: a + b, [t.astype(f32) for t in terms])


def add_low(whole, part, axis):
    low, high = jnp.split(whole, 2, axis)
    return jnp.concatenate([add(low, part).astype(bf16), high], axis=axis)


def add_high(whole, part, axis):
    low, high = jnp.split(whole, 2, axis)
    return jnp.concatenate([low, add(high, part).astype(bf16)], axis=axis)


def couple(results, others):
    return lax.optimization_barrier((tuple(results), tuple(others)))[0]


def reduce_weights(ring, near, far, extra):
    z_res = (z_shift(ring[4, :1], 1), z_shift(ring[4, 1:], -1))
    x_res = (swap_a(far[1, 0, :, :1]), swap_b(far[1, 0, :, 1:]))
    w, v = z_res
    z_send = (add_low(ring[3], w, 0), add_high(ring[5], v, 0))
    x_res = couple(x_res, z_send)
    x_send = (add_high(far[0, 1], x_res[1], 1), add_low(far[1, 1], x_res[0], 1))
    z_res = couple((z_shift(z_send[0], 1), z_shift(z_send[1], -1)), x_send)
    x_res = (swap_a(x_send[0]), swap_b(x_send[1]))
    z_send = (add(ring[2], z_res[0]).astype(bf16), add(ring[6], z_res[1]).astype(bf16))
    x_res = couple(x_res, z_send + tuple(extra))
    far_sum = add(far[0, 0], *x_res).astype(bf16)
    x_send = (near[1, 0, :, :1], near[1, 0, :, 1:])
    x_send = couple(x_send, (far_sum,))
    z_res = couple((z_shift(z_send[0], 1), z_shift(z_send[1], -1)), x_send)
    n_res = (z_shift(far_sum[1, :1], 1), z_shift(far_sum[1, 1:], -1))
    x_res = (swap_a(x_send[0]), swap_b(x_send[1]))
    z_send = (add(ring[1], z_res[0]).astype(bf16), add(ring[7], z_res[1]).astype(bf16))
    n_send = (add_low(far_sum[0], n_res[0], 0), add_high(far_sum[2], n_res[1], 0))
    x_res = couple(x_res, z_send + n_send)
    x_send = (add_high(near[0, 1], x_res[1], 1), add_low(near[1, 1], x_res[0], 1))
    z_res = couple((z_shift(z_send[0], 1), z_shift(z_send[1], -1)), x_send)
    n_res = couple((z_shift(n_send[0], 1), z_shift(n_send[1], -1)), x_send)
    x_res = (swap_a(x_send[0]), swap_b(x_send[1]))
    ring_sum = add(ring[0], *z_res).astype(bf16)
    x_res = couple(x_res, (ring_sum,))
    near_sum = add(near[0, 0], *x_res).astype(bf16)
    n_send = (add(near_sum[2], n_res[0]).astype(bf16), add(near_sum[3], n_res[1]).astype(bf16))
    n_res = (z_shift(n_send[0], 1), z_shift(n_send[1], -1))
    x_res = (swap_a(ring_sum[1, 0, :1]), swap_b(ring_sum[1, 0, 1:]))
    x_send = (add_high(ring_sum[0, 1], x_res[1], 0), add_low(ring_sum[1, 1], x_res[0], 0))
    n_res = couple(n_res, x_send)
    n_send = (add(near_sum[1], n_res[0]).astype(bf16), add(near_sum[4], n_res[1]).astype(bf16))
    x_res = (swap_a(x_send[0]), swap_b(x_send[1]))
    n_res = (z_shift(n_send[0], 1), z_shift(n_send[1], -1))
    return jnp.concatenate(
        [add(ring_sum[0, 0], *x_res), add(near_sum[0], *n_res)], axis=-1
    )


def norm_of(codes):
    values = codes.astype(f32)
    scales = lax.rsqrt(jnp.mean(values * values, axis=-1, keepdims=True) + eps)
    return values, scales


def grad_through_norm(grad_out, codes, left, right):
    values, scales = norm_of(codes)
    summed = left.astype(f32) + right.astype(f32)
    inner = jnp.mean(summed * values, axis=-1, keepdims=True)
    return (
        grad_out.astype(f32) + scales * summed - values * (scales * scales * scales) * inner
    )


def dot_rows(left, right):
    return lax.dot_general(left, right, (((1,), (0,)), ((), ())), preferred_element_type=f32)


def dot_last(left, right):
    return lax.dot_general(left, right, (((1,), (1,)), ((), ())), preferred_element_type=f32)


def dot_first(left, right):
    return lax.dot_general(left, right, (((0,), (0,)), ((), ())), preferred_element_type=f32)


def forward_kernel(n_terms, keep, *refs):
    terms, weight_ref, outs = refs[:n_terms], refs[n_terms], refs[n_terms + 1 :]
    code_ref, part_ref = outs[:2]
    codes = terms[1][...].astype(f32)
    if n_terms == 3:
        codes = codes + terms[2][...].astype(f32)
    codes = (terms[0][...].astype(f32) + codes).astype(bf16)
    code_ref[...] = codes
    values, scales = norm_of(codes)
    normed = (values * scales).astype(bf16)
    total = None
    for low in range(0, COLS, TILE):
        span = slice(low, low + TILE)
        half = 0.5 * dot_rows(normed, weight_ref[0, :, span])
        bend = jnp.tanh(half)
        gated = (half + half * bend).astype(bf16)
        if keep:
            outs[2][:, span] = gated
            outs[3][:, span] = (0.5 * (1.0 + bend) * (1.0 + half * (1.0 - bend))).astype(bf16)
        part = dot_last(gated, weight_ref[1, :, span])
        total = part if total is None else total + part
    part_ref[...] = total.astype(bf16)


def section_cost(rows):
    return pl.CostEstimate(
        flops=4 * rows * WIDTH * COLS,
        bytes_accessed=4 * WIDTH * COLS + 8 * rows * WIDTH,
        transcendentals=rows * COLS,
    )


def section_forward(terms, weights, keep):
    rows = terms[0].shape[0]
    out_shape = [jax.ShapeDtypeStruct((rows, WIDTH), bf16)] * 2
    if keep:
        out_shape += [jax.ShapeDtypeStruct((rows, COLS), bf16)] * 2
    return pl.pallas_call(
        functools.partial(forward_kernel, len(terms), keep),
        out_shape=out_shape,
        compiler_params=pltpu.CompilerParams(vmem_limit_bytes=24 * MIB),
        cost_estimate=section_cost(rows),
    )(*terms, weights)


def backward_kernel(n_terms, keep, *refs):
    terms, slope_ref, weight_ref = refs[:n_terms], refs[n_terms], refs[n_terms + 1]
    outs = refs[n_terms + 2 :]
    grad_ref, part_ref = outs[:2]
    if n_terms == 2:
        grad = terms[0][...].astype(f32) + terms[1][...].astype(f32)
    else:
        grad = grad_through_norm(*[t[...] for t in terms])
        if keep:
            outs[3][...] = grad
    grad = grad.astype(bf16)
    grad_ref[...] = grad
    total = None
    for low in range(0, COLS, TILE):
        span = slice(low, low + TILE)
        gated_grad = dot_rows(grad, weight_ref[1, :, span])
        hidden_grad = (gated_grad * slope_ref[:, span].astype(f32)).astype(bf16)
        if keep:
            outs[2][:, span] = hidden_grad
        part = dot_last(hidden_grad, weight_ref[0, :, span])
        total = part if total is None else total + part
    part_ref[...] = total.astype(bf16)


def section_backward(terms, slope, weights, keep):
    rows = terms[0].shape[0]
    out_shape = [jax.ShapeDtypeStruct((rows, WIDTH), bf16)] * 2
    if keep:
        out_shape += [jax.ShapeDtypeStruct((rows, COLS), bf16)]
        if len(terms) > 2:
            out_shape += [jax.ShapeDtypeStruct((rows, WIDTH), f32)]
    return pl.pallas_call(
        functools.partial(backward_kernel, len(terms), keep),
        out_shape=out_shape,
        compiler_params=pltpu.CompilerParams(vmem_limit_bytes=24 * MIB),
        cost_estimate=section_cost(rows),
    )(*terms, slope, weights)


def norm_grad_kernel(grad_ref, code_ref, left_ref, right_ref, out_ref):
    out_ref[...] = grad_through_norm(
        grad_ref[...], code_ref[...], left_ref[...], right_ref[...]
    ).astype(out_ref.dtype)


def norm_grad(grad, codes, left, right, dtype):
    return pl.pallas_call(
        norm_grad_kernel, out_shape=jax.ShapeDtypeStruct(grad.shape, dtype)
    )(grad, codes, left, right)


def seed_kernel(flag_ref, lengths_ref, code_ref, left_ref, right_ref, head_ref, out_ref):
    codes = (
        code_ref[...].astype(f32) + (left_ref[...].astype(f32) + right_ref[...].astype(f32))
    ).astype(bf16)
    head = head_ref[...].astype(f32)
    scores = jnp.sum(codes.astype(f32) * head, axis=-1, keepdims=True)
    rows = scores.shape[0]
    seq_len = rows // 2
    position = lax.broadcasted_iota(jnp.int32, (rows, 1), 0)
    chosen_length, other_length = lengths_ref[0], lengths_ref[1]
    chosen = jnp.where(position < seq_len, 1.0, 0.0)
    limit = jnp.where(position < seq_len, chosen_length, other_length + seq_len)
    valid = jnp.where(position < limit, 1.0, 0.0)
    chosen_count = jnp.full((1, 1), chosen_length, jnp.int32).astype(f32)
    other_count = jnp.full((1, 1), other_length, jnp.int32).astype(f32)
    chosen_sum = jnp.sum(scores * valid * chosen, axis=0, keepdims=True)
    other_sum = jnp.sum(scores * valid * (1.0 - chosen), axis=0, keepdims=True)
    gap = other_sum / other_count - chosen_sum / chosen_count
    weight = loss_scale * jax.nn.sigmoid(gap)
    token = (1.0 - chosen) * (weight / other_count) - chosen * (weight / chosen_count)
    token = token * valid * jnp.full((1, 1), flag_ref[0], jnp.int32).astype(f32)
    out_ref[...] = (token * head).astype(bf16)


def reward_seed(flag, lengths, codes, left, right, head):
    vmem = pl.BlockSpec(memory_space=pltpu.VMEM)
    smem = pl.BlockSpec(memory_space=pltpu.SMEM)
    return pl.pallas_call(
        seed_kernel,
        in_specs=[smem, smem, vmem, vmem, vmem, vmem],
        out_specs=vmem,
        out_shape=jax.ShapeDtypeStruct(codes.shape, bf16),
    )(flag, lengths, codes, left, right, head)


def weight_grad_kernel(*refs):
    grads, codes = refs[0:CHUNKS], refs[CHUNKS : 2 * CHUNKS]
    gated, hidden = refs[2 * CHUNKS : 3 * CHUNKS], refs[3 * CHUNKS : 4 * CHUNKS]
    ring_ref, near_ref, far_ref = refs[-3:]

    def joined(group):
        return jnp.concatenate([ref[...] for ref in group], axis=0)

    values, scales = norm_of(joined(codes))
    normed = (values * scales).astype(bf16)
    for mat, (left, group) in enumerate(((normed, hidden), (joined(grads), gated))):
        for low, high in ((0, XPART), (XPART, SPAN)):
            right = jnp.concatenate([ref[:, low:high] for ref in group], axis=0)
            result = dot_first(left, right).astype(bf16)
            for xr in range(2):
                for dz in range(Z):
                    row = (xr * Z + dz) * SUB
                    piece = result[row : row + SUB]
                    if low == 0:
                        ring_ref[dz, 0, xr, 0, mat] = piece
                    elif dz in NEAR:
                        near_ref[0, xr, NEAR.index(dz), 0, mat] = piece
                    else:
                        far_ref[0, xr, FAR.index(dz), 0, mat] = piece


def weight_grads(section, grads, codes, gated, hidden, held):
    rows = grads[0].shape[0]
    narrow = pl.BlockSpec((rows, WIDTH), lambda t: (0, 0))
    wide = pl.BlockSpec((rows, SPAN), lambda t: (0, t))
    n_in = 4 * CHUNKS

    def group_spec(count):
        return pl.BlockSpec(
            (1, 2, count, 1, 2, SUB, ZPART), lambda t: (t, 0, 0, section, 0, 0, 0)
        )

    return pl.pallas_call(
        weight_grad_kernel,
        grid=(2,),
        in_specs=[narrow] * (2 * CHUNKS)
        + [wide] * (2 * CHUNKS)
        + [pl.BlockSpec(memory_space=pl.ANY)] * len(held),
        out_specs=[
            pl.BlockSpec((Z, 1, 2, 1, 2, SUB, XPART), lambda t: (0, t, 0, section, 0, 0, 0)),
            group_spec(len(NEAR)),
            group_spec(len(FAR)),
        ],
        out_shape=[
            jax.ShapeDtypeStruct((Z, 2, 2, 2, 2, SUB, XPART), bf16),
            jax.ShapeDtypeStruct((2, 2, len(NEAR), 2, 2, SUB, ZPART), bf16),
            jax.ShapeDtypeStruct((2, 2, len(FAR), 2, 2, SUB, ZPART), bf16),
        ],
        input_output_aliases={n_in + k: k for k in range(len(held))},
        compiler_params=pltpu.CompilerParams(vmem_limit_bytes=40 * MIB),
        cost_estimate=pl.CostEstimate(
            flops=8 * rows * CHUNKS * WIDTH * COLS // 2,
            bytes_accessed=4 * WIDTH * COLS,
            transcendentals=0,
        ),
    )(*grads, *codes, *gated, *hidden, *held)


def to_local(value, pair, z_index):
    lead = value.shape[:-1]
    value = value.reshape(lead + (2, Z, SUB))
    axis = len(lead)
    value = jnp.where(pair == 0, value, jnp.flip(value, axis))
    doubled = jnp.concatenate([value, value], axis=axis + 1)
    return lax.dynamic_slice_in_dim(doubled, z_index, Z, axis + 1).reshape(lead + (WIDTH,))


def to_global(value, pair, z_index):
    return to_local(value, pair, (Z - z_index) % Z)


def on_device(codes_in, lengths, dec_weight, enc_weight, head):
    pipe = lax.axis_index("pipe")
    core, stage = pipe % 2, pipe // 2
    tensor = lax.axis_index("tensor")
    dp = lax.axis_index("dp")
    pair, z_index = dp // Z, dp % Z

    weights = gather_weights(dec_weight, enc_weight, core)

    codes_in = lax.dynamic_slice_in_dim(codes_in, tensor * CHUNKS, CHUNKS, 0)
    lengths = lax.dynamic_slice_in_dim(lengths, tensor * CHUNKS, CHUNKS, 0)
    codes_in = to_local(codes_in, pair, z_index)
    codes_in = jnp.where(stage == 0, codes_in, jnp.zeros_like(codes_in))
    head = to_local(head[None], pair, z_index)
    is_last = (stage == STAGES - 1).astype(jnp.int32)[None]

    rows = codes_in.shape[1]
    blank = jnp.zeros((rows, WIDTH), bf16)
    chunks = range(CHUNKS)
    received = [blank] * CHUNKS
    codes = [[None, None] for _ in chunks]
    gated = [[None, None] for _ in chunks]
    slope = [[None, None] for _ in chunks]
    seeds = [None] * CHUNKS
    for step in range(STAGES):
        keep = step == STAGES - 1
        for m in chunks:
            first = section_forward([received[m], codes_in[m]], weights[0], keep)
            second = section_forward([first[0], first[1], core_swap(first[1])], weights[1], keep)
            across = core_swap(second[1])
            if keep:
                codes[m] = [first[0], second[0]]
                gated[m] = [first[2], second[2]]
                slope[m] = [first[3], second[3]]
                seeds[m] = reward_seed(is_last, lengths[m], second[0], second[1], across, head)
            else:
                received[m] = y_shift(add(second[0], add(second[1], across)).astype(bf16), 1)

    received = [blank] * CHUNKS
    grads = [[None] * CHUNKS, [None] * CHUNKS]
    hidden = [[None] * CHUNKS, [None] * CHUNKS]
    through = [[None] * CHUNKS, [None] * CHUNKS]
    for step in range(STAGES):
        keep = step == STAGES - 1
        for m in chunks:
            second = section_backward([received[m], seeds[m]], slope[m][1], weights[1], keep)
            second_across = core_swap(second[1])
            first = section_backward(
                [second[0], codes[m][1], second[1], second_across], slope[m][0], weights[0], keep
            )
            first_across = core_swap(first[1])
            passed = norm_grad(
                first[0], codes[m][0], first[1], first_across, f32 if keep else bf16
            )
            if keep:
                grads[0][m], grads[1][m] = first[0], second[0]
                hidden[0][m], hidden[1][m] = first[2], second[2]
                through[0][m], through[1][m] = passed, first[3]
            else:
                received[m] = y_shift(passed, -1)

    held = ()
    for section in (1, 0):
        held = weight_grads(
            section,
            grads[section],
            [codes[m][section] for m in chunks],
            [gated[m][section] for m in chunks],
            hidden[section],
            held,
        )

    code_grads = jnp.where(core == 0, jnp.stack(through[0]), jnp.stack(through[1]))
    code_grads = to_global(code_grads, pair, z_index)
    share = rows // 2
    kept = lax.dynamic_slice_in_dim(code_grads, tensor * share, share, 1)
    sent = lax.dynamic_slice_in_dim(code_grads, (1 - tensor) * share, share, 1)
    got = lax.ppermute(sent.astype(bf16), "tensor", [(0, 1), (1, 0)])
    summed = reduce_weights(*held, (got,))
    got = got.astype(f32)
    code_out = jnp.where(
        tensor == 0, jnp.concatenate([kept, got], axis=0), jnp.concatenate([got, kept], axis=0)
    )

    mine = lax.dynamic_index_in_dim(summed, core, 0, keepdims=False)
    other = core_swap(lax.dynamic_index_in_dim(summed, 1 - core, 0, keepdims=False))
    full = jnp.where(
        core == 0,
        jnp.concatenate([mine, other], axis=-1),
        jnp.concatenate([other, mine], axis=-1),
    )
    return (code_out[None], full[0][None], full[1][None])


def solution(mesh):
    in_specs = (
        P(None, "dp", None),
        P(None, "dp"),
        P("pipe", "dp", "tensor"),
        P("pipe", "dp", "tensor"),
        P(),
    )
    out_specs = (
        P("pipe", None, ("dp", "tensor"), None),
        P("pipe", "dp", "tensor"),
        P("pipe", "dp", "tensor"),
    )
    return jax.shard_map(
        on_device, mesh=mesh, in_specs=in_specs, out_specs=out_specs, check_vma=False
    )
```

```python
import functools

import jax
import jax.numpy as jnp
from jax import lax
from jax.experimental import pallas as pl
from jax.experimental.pallas import tpu as pltpu
from jax.sharding import PartitionSpec as P

eps = 1e-05
loss_scale = 512.0
f32 = jnp.float32
bf16 = jnp.bfloat16

Z = 8
SUB = 32
WIDTH = 512
SPAN = 2048
COLS = 4096
XPART = 896
ZPART = SPAN - XPART
TILE = 1024
NEAR = (0, 1, 2, 6, 7)
FAR = (3, 4, 5)
CLOSE = (0, 1, 7)
DISTANT = (2, 3, 4, 5, 6)
MIB = 1024 * 1024
CHUNKS = 2
STAGES = 4


def core_swap(value):
    return lax.ppermute(value, "pipe", [(i, i ^ 1) for i in range(8)])


def y_shift(value, steps):
    return lax.ppermute(
        value, "pipe", [(i, i + 2 * steps) for i in range(8) if 0 <= i + 2 * steps < 8]
    )


def z_shift(value, steps):
    return lax.ppermute(
        value, "dp", [(x * Z + z, x * Z + (z + steps) % Z) for x in range(2) for z in range(Z)]
    )


def swap_a(value):
    return lax.ppermute(value, "dp", [(x * Z + z, (1 - x) * Z + z) for x in range(2) for z in range(Z)])


def swap_b(value):
    pairs = [
        ((x * Z + z) * 2 + t, ((1 - x) * Z + z) * 2 + 1 - t)
        for x in range(2)
        for z in range(Z)
        for t in range(2)
    ]
    return lax.ppermute(value, ("dp", "tensor"), pairs)


def fenced(*values):
    return lax.optimization_barrier(values)


def copy_kernel(moves, n_in, *refs):
    sources, targets, sems = refs[:n_in], refs[-5:-1], refs[-1]
    copies = []
    for k, (which, src, target, dst) in enumerate(moves):
        copy = pltpu.make_async_copy(
            sources[which].at[src], targets[target].at[dst], sems.at[k]
        )
        copy.start()
        copies.append(copy)
    for copy in copies:
        copy.wait()


def place(pieces, moves, held):
    vmem = pl.BlockSpec(memory_space=pltpu.VMEM)
    n_in = len(pieces)
    return pl.pallas_call(
        functools.partial(copy_kernel, moves, n_in),
        out_shape=[jax.ShapeDtypeStruct((WIDTH, COLS), bf16)] * 4,
        in_specs=[pl.BlockSpec(memory_space=pl.ANY)] * n_in + [vmem] * len(held),
        out_specs=[vmem] * 4,
        scratch_shapes=[pltpu.SemaphoreType.DMA((len(moves),))],
        input_output_aliases={n_in + k: k for k in range(len(held))},
        compiler_params=pltpu.CompilerParams(vmem_limit_bytes=24 * MIB),
        cost_estimate=pl.CostEstimate(
            flops=0, bytes_accessed=8 * WIDTH * COLS, transcendentals=0
        ),
    )(*pieces, *held)


def spot(xr, dz, tr, low, high):
    row = (xr * Z + dz) * SUB
    return (slice(row, row + SUB), slice(tr * SPAN + low, tr * SPAN + high))


def narrow_moves(group, blocks, pieces, moves):
    for section in range(2):
        for (tr, xr), block in zip(((0, 0), (0, 1), (1, 1), (1, 0)), blocks[section]):
            for k, dz in enumerate(group):
                for mat in range(2):
                    moves.append(
                        (len(pieces), (k, mat), 2 * section + mat, spot(xr, dz, tr, XPART, SPAN))
                    )
            pieces.append(block)


def ring_moves(dz, halves, pieces, moves):
    for section in range(2):
        for mat in range(2):
            for tr in range(2):
                for xr in range(2):
                    which, index = (tr, 0) if len(halves) == 2 else (0, tr)
                    moves.append(
                        (
                            len(pieces) + which,
                            (index, xr, section, mat),
                            2 * section + mat,
                            spot(xr, dz, tr, 0, XPART),
                        )
                    )
    pieces.extend(halves)


def gather_weights(dec_weight, enc_weight, core):
    own = jnp.stack([dec_weight[0], enc_weight[0]])
    mine = lax.dynamic_slice_in_dim(own, core * SPAN, SPAN, 2)
    other = core_swap(lax.dynamic_slice_in_dim(own, (1 - core) * SPAN, SPAN, 2))
    first = core == 0
    block = jnp.stack([jnp.where(first, mine, other), jnp.where(first, other, mine)])
    part_x, part_z = block[..., :XPART], block[..., XPART:]

    a, b, u1, d1 = fenced(
        swap_a(part_x), swap_b(part_x), z_shift(part_z, 1), z_shift(part_z, -1)
    )
    da, db, u2, d2 = fenced(swap_a(b[:1]), swap_b(a[1:]), z_shift(u1, 1), z_shift(d1, -1))
    ring = jnp.stack(
        [jnp.stack([part_x, a]), jnp.stack([jnp.concatenate([da, db], axis=0), b])]
    )
    near = [jnp.stack([t[s] for t in (part_z, d1, d2, u2, u1)]) for s in range(2)]
    w1, v1, near_a1, near_b0, u3, d3, near_a0, near_b1 = fenced(
        z_shift(ring, 1),
        z_shift(ring, -1),
        swap_a(near[1]),
        swap_b(near[0]),
        z_shift(u2, 1),
        z_shift(d2, -1),
        swap_a(near[0]),
        swap_b(near[1]),
    )
    w2, v2, near_d0, near_d1, u4, d4 = fenced(
        z_shift(w1, 1),
        z_shift(v1, -1),
        swap_a(near_b0),
        swap_b(near_a1),
        z_shift(u3[:1], 1),
        z_shift(d3[1:], -1),
    )
    far = [jnp.stack([d3[0], u4[0], u3[0]]), jnp.stack([d3[1], d4[0], u3[1]])]
    w3, v3, far_a1, far_b0, far_a0, far_b1 = fenced(
        z_shift(w2, 1),
        z_shift(v2, -1),
        swap_a(far[1]),
        swap_b(far[0]),
        swap_a(far[0]),
        swap_b(far[1]),
    )
    w4, v4 = z_shift(w3[:1], 1), z_shift(v3[1:], -1)
    far_d0, far_d1 = swap_a(far_b0), swap_b(far_a1)

    pieces, moves = [], []
    narrow_moves(
        NEAR,
        ((near[0], near_a0, near_b0, near_d0), (near[1], near_a1, near_b1, near_d1)),
        pieces,
        moves,
    )
    for dz, piece in ((0, ring), (1, v1), (7, w1), (2, v2), (6, w2)):
        ring_moves(dz, [piece], pieces, moves)
    held = place(pieces, moves, ())
    pieces, moves = [], []
    narrow_moves(
        FAR,
        ((far[0], far_a0, far_b0, far_d0), (far[1], far_a1, far_b1, far_d1)),
        pieces,
        moves,
    )
    ring_moves(3, [v3], pieces, moves)
    ring_moves(5, [w3], pieces, moves)
    ring_moves(4, [w4, v4], pieces, moves)
    dec_0, enc_0, dec_1, enc_1 = place(pieces, moves, held)
    return ((dec_0, enc_0), (dec_1, enc_1))


def add(*terms):
    return functools.reduce(lambda a, b: a + b, [t.astype(f32) for t in terms])


def add16(*terms):
    return add(*terms).astype(bf16)


def couple(results, others):
    return lax.optimization_barrier((tuple(results), tuple(others)))[0]


CHAINS = {(0, 1): (4, 3, 2, 1), (0, -1): (5, 6, 7), (1, 1): (3, 2, 1), (1, -1): (4, 5, 6, 7)}


def first_swap(section, value):
    return swap_a(value) if section == 0 else swap_b(value)


def second_swap(section, value):
    return swap_b(value) if section == 0 else swap_a(value)


class ZChain:
    def __init__(self, piece):
        self.piece = piece
        self.step = 0
        self.done = {}
        self.send = {key: piece(key[0], dzs[0]) for key, dzs in CHAINS.items()}

    def shift(self):
        self.result = {key: z_shift(value, key[1]) for key, value in self.send.items()}

    def merge(self):
        self.step += 1
        self.send = {}
        for key, value in self.result.items():
            if self.step < len(CHAINS[key]):
                self.send[key] = add16(self.piece(key[0], CHAINS[key][self.step]), value)
            else:
                self.done[key] = value
        return tuple(self.send.values())


def reduce_weights(parts, code_exchange):
    sections = (0, 1)
    ring = [part[:Z] for part in parts]
    far = [part[Z : Z + 3] for part in parts]
    near = [part[Z + 3 :] for part in parts]

    wide = ZChain(lambda s, dz: ring[s][dz])
    wide.shift()
    far_1 = [first_swap(s, far[s][0]) for s in sections]
    made = wide.merge()
    far_1 = couple(far_1, made)
    far_send = [add16(far[s][1], far_1[s][0]) for s in sections]

    wide.shift()
    far_2 = [second_swap(s, far_send[s]) for s in sections]
    near_1 = [first_swap(s, near[s][0]) for s in sections]
    made = wide.merge()
    far_2 = couple(far_2, made)
    near_2 = None
    near_sums = {}

    def narrow_piece(s, dz):
        if dz in DISTANT:
            k = DISTANT.index(dz)
            return add16(far[s][2][k], far_1[s][1, k], far_2[s][k])
        k = CLOSE.index(dz)
        return add16(near[s][2][k], near_1[s][1, k], near_2[s][k])

    narrow = ZChain(narrow_piece)
    wide.shift()
    narrow.shift()
    made = wide.merge()
    near_1 = couple(near_1, made)
    near_send = [add16(near[s][1], near_1[s][0]) for s in sections]
    near_2 = [second_swap(s, near_send[s]) for s in sections]
    made = narrow.merge()
    near_2 = couple(near_2, made)

    wide.shift()
    narrow.shift()
    wide.merge()

    def ring_sum(s, span, *more):
        return add(ring[s][0][span], wide.done[s, 1][span], wide.done[s, -1][span], *more)

    ring_first = [ring_sum(s, slice(0, 2)).astype(bf16) for s in sections]
    ring_1 = [first_swap(s, ring_first[s]) for s in sections]
    made = narrow.merge()
    narrow.shift()
    got = code_exchange(made)
    ring_1 = couple(ring_1, made)
    ring_send = [ring_sum(s, 2, ring_1[s][0]).astype(bf16) for s in sections]
    ring_2 = [second_swap(s, ring_send[s]) for s in sections]
    narrow.merge()
    narrow.shift()
    narrow.merge()
    sums = []
    for s in sections:
        k = CLOSE.index(0)
        last = add(
            near[s][2][k], near_1[s][1, k], near_2[s][k], narrow.done[s, 1], narrow.done[s, -1]
        )
        sums.append(jnp.concatenate([ring_sum(s, 3, ring_1[s][1], ring_2[s]), last], axis=-1))
    return sums, got


def norm_of(codes):
    values = codes.astype(f32)
    scales = lax.rsqrt(jnp.mean(values * values, axis=-1, keepdims=True) + eps)
    return values, scales


def grad_through_norm(grad_out, codes, left, right):
    values, scales = norm_of(codes)
    summed = left.astype(f32) + right.astype(f32)
    inner = jnp.mean(summed * values, axis=-1, keepdims=True)
    return (
        grad_out.astype(f32) + scales * summed - values * (scales * scales * scales) * inner
    )


def dot_rows(left, right):
    return lax.dot_general(left, right, (((1,), (0,)), ((), ())), preferred_element_type=f32)


def dot_last(left, right):
    return lax.dot_general(left, right, (((1,), (1,)), ((), ())), preferred_element_type=f32)


def dot_first(left, right):
    return lax.dot_general(left, right, (((0,), (0,)), ((), ())), preferred_element_type=f32)


def start_tiles(source, target, sems):
    copies = []
    for k, low in enumerate(range(0, COLS, TILE)):
        span = slice(low, low + TILE)
        copy = pltpu.make_async_copy(source.at[:, span], target.at[:, span], sems.at[k])
        copy.start()
        copies.append(copy)
    return copies


def forward_kernel(n_terms, keep, *refs):
    terms, (dec_ref, enc_hbm), outs = refs[:n_terms], refs[n_terms : n_terms + 2], refs[n_terms + 2 :]
    enc_ref, enc_sems = outs[-2:]
    enc_copies = start_tiles(enc_hbm, enc_ref, enc_sems)
    code_ref, part_ref = outs[:2]
    codes = terms[1][...].astype(f32)
    if n_terms == 3:
        codes = codes + terms[2][...].astype(f32)
    codes = (terms[0][...].astype(f32) + codes).astype(bf16)
    code_ref[...] = codes
    values, scales = norm_of(codes)
    normed = (values * scales).astype(bf16)
    total = None
    for k, low in enumerate(range(0, COLS, TILE)):
        span = slice(low, low + TILE)
        half = 0.5 * dot_rows(normed, dec_ref[:, span])
        bend = jnp.tanh(half)
        gated = (half + half * bend).astype(bf16)
        if keep:
            outs[2][:, span] = gated
            outs[3][:, span] = (0.5 * (1.0 + bend) * (1.0 + half * (1.0 - bend))).astype(bf16)
        enc_copies[k].wait()
        part = dot_last(gated, enc_ref[:, span])
        total = part if total is None else total + part
    part_ref[...] = total.astype(bf16)


def section_cost(rows):
    return pl.CostEstimate(
        flops=4 * rows * WIDTH * COLS,
        bytes_accessed=4 * WIDTH * COLS + 8 * rows * WIDTH,
        transcendentals=rows * COLS,
    )


def tile_scratch(rows):
    return [pltpu.VMEM((rows, COLS), bf16), pltpu.SemaphoreType.DMA((COLS // TILE,))]


def section_forward(terms, weights, keep):
    rows = terms[0].shape[0]
    vmem, hbm = pl.BlockSpec(memory_space=pltpu.VMEM), pl.BlockSpec(memory_space=pl.ANY)
    out_shape = [jax.ShapeDtypeStruct((rows, WIDTH), bf16)] * 2
    if keep:
        out_shape += [jax.ShapeDtypeStruct((rows, COLS), bf16)] * 2
    return pl.pallas_call(
        functools.partial(forward_kernel, len(terms), keep),
        in_specs=[vmem] * (len(terms) + 1) + [hbm],
        out_specs=[vmem] * len(out_shape),
        out_shape=out_shape,
        scratch_shapes=tile_scratch(WIDTH),
        compiler_params=pltpu.CompilerParams(vmem_limit_bytes=24 * MIB),
        cost_estimate=section_cost(rows),
    )(*terms, *weights)


def backward_kernel(n_terms, keep, *refs):
    terms, (dec_ref, enc_hbm, slope_hbm) = refs[:n_terms], refs[n_terms : n_terms + 3]
    outs = refs[n_terms + 3 :]
    enc_ref, enc_sems, slope_ref, slope_sems = outs[-4:]
    enc_copies = start_tiles(enc_hbm, enc_ref, enc_sems)
    slope_copies = start_tiles(slope_hbm, slope_ref, slope_sems)
    grad_ref, part_ref = outs[:2]
    if n_terms == 2:
        grad = terms[0][...].astype(f32) + terms[1][...].astype(f32)
    else:
        grad = grad_through_norm(*[t[...] for t in terms])
        if keep:
            outs[3][...] = grad
    grad = grad.astype(bf16)
    grad_ref[...] = grad
    total = None
    for k, low in enumerate(range(0, COLS, TILE)):
        span = slice(low, low + TILE)
        enc_copies[k].wait()
        gated_grad = dot_rows(grad, enc_ref[:, span])
        slope_copies[k].wait()
        hidden_grad = (gated_grad * slope_ref[:, span].astype(f32)).astype(bf16)
        if keep:
            outs[2][:, span] = hidden_grad
        part = dot_last(hidden_grad, dec_ref[:, span])
        total = part if total is None else total + part
    part_ref[...] = total.astype(bf16)


def section_backward(terms, slope, weights, keep):
    rows = terms[0].shape[0]
    vmem, hbm = pl.BlockSpec(memory_space=pltpu.VMEM), pl.BlockSpec(memory_space=pl.ANY)
    out_shape = [jax.ShapeDtypeStruct((rows, WIDTH), bf16)] * 2
    if keep:
        out_shape += [jax.ShapeDtypeStruct((rows, COLS), bf16)]
        if len(terms) > 2:
            out_shape += [jax.ShapeDtypeStruct((rows, WIDTH), f32)]
    return pl.pallas_call(
        functools.partial(backward_kernel, len(terms), keep),
        in_specs=[vmem] * (len(terms) + 1) + [hbm, hbm],
        out_specs=[vmem] * len(out_shape),
        out_shape=out_shape,
        scratch_shapes=tile_scratch(WIDTH) + tile_scratch(rows),
        compiler_params=pltpu.CompilerParams(vmem_limit_bytes=24 * MIB),
        cost_estimate=section_cost(rows),
    )(*terms, *weights, slope)


def norm_grad_kernel(grad_ref, code_ref, left_ref, right_ref, out_ref):
    out_ref[...] = grad_through_norm(
        grad_ref[...], code_ref[...], left_ref[...], right_ref[...]
    ).astype(out_ref.dtype)


def norm_grad(grad, codes, left, right, dtype):
    return pl.pallas_call(
        norm_grad_kernel, out_shape=jax.ShapeDtypeStruct(grad.shape, dtype)
    )(grad, codes, left, right)


def seed_kernel(flag_ref, lengths_ref, code_ref, left_ref, right_ref, head_ref, out_ref):
    codes = (
        code_ref[...].astype(f32) + (left_ref[...].astype(f32) + right_ref[...].astype(f32))
    ).astype(bf16)
    head = head_ref[...].astype(f32)
    scores = jnp.sum(codes.astype(f32) * head, axis=-1, keepdims=True)
    rows = scores.shape[0]
    seq_len = rows // 2
    position = lax.broadcasted_iota(jnp.int32, (rows, 1), 0)
    chosen_length, other_length = lengths_ref[0], lengths_ref[1]
    chosen = jnp.where(position < seq_len, 1.0, 0.0)
    limit = jnp.where(position < seq_len, chosen_length, other_length + seq_len)
    valid = jnp.where(position < limit, 1.0, 0.0)
    chosen_count = jnp.full((1, 1), chosen_length, jnp.int32).astype(f32)
    other_count = jnp.full((1, 1), other_length, jnp.int32).astype(f32)
    chosen_sum = jnp.sum(scores * valid * chosen, axis=0, keepdims=True)
    other_sum = jnp.sum(scores * valid * (1.0 - chosen), axis=0, keepdims=True)
    gap = other_sum / other_count - chosen_sum / chosen_count
    weight = loss_scale * jax.nn.sigmoid(gap)
    token = (1.0 - chosen) * (weight / other_count) - chosen * (weight / chosen_count)
    token = token * valid * jnp.full((1, 1), flag_ref[0], jnp.int32).astype(f32)
    out_ref[...] = (token * head).astype(bf16)


def reward_seed(flag, lengths, codes, left, right, head):
    vmem = pl.BlockSpec(memory_space=pltpu.VMEM)
    smem = pl.BlockSpec(memory_space=pltpu.SMEM)
    return pl.pallas_call(
        seed_kernel,
        in_specs=[smem, smem, vmem, vmem, vmem, vmem],
        out_specs=vmem,
        out_shape=jax.ShapeDtypeStruct(codes.shape, bf16),
    )(flag, lengths, codes, left, right, head)


def weight_grad_kernel(order, *refs):
    grads, codes = refs[0:CHUNKS], refs[CHUNKS : 2 * CHUNKS]
    gated, hidden = refs[2 * CHUNKS : 3 * CHUNKS], refs[3 * CHUNKS : 4 * CHUNKS]
    outs = refs[4 * CHUNKS :]
    ring_refs, far_refs, near_refs = outs[:Z], outs[Z : Z + 3], outs[Z + 3 :]

    def joined(group):
        return jnp.concatenate([ref[...] for ref in group], axis=0)

    values, scales = norm_of(joined(codes))
    normed = (values * scales).astype(bf16)
    for mat, (left, group) in enumerate(((normed, hidden), (joined(grads), gated))):
        for tr in range(2):
            for low, high in ((0, XPART), (XPART, SPAN)):
                span = slice(tr * SPAN + low, tr * SPAN + high)
                right = jnp.concatenate([ref[:, span] for ref in group], axis=0)
                result = dot_first(left, right).astype(bf16)
                for xr in range(2):
                    place_at = order.index((tr, xr))
                    for dz in range(Z):
                        row = (xr * Z + dz) * SUB
                        piece = result[row : row + SUB]
                        if low == 0:
                            ring_refs[dz][place_at, mat] = piece
                            continue
                        group_refs, k = (
                            (far_refs, DISTANT.index(dz))
                            if dz in DISTANT
                            else (near_refs, CLOSE.index(dz))
                        )
                        if place_at < 2:
                            group_refs[0][place_at, k, mat] = piece
                        else:
                            group_refs[place_at - 1][k, mat] = piece


def weight_grads(section, grads, codes, gated, hidden):
    order = ((1, 0), (0, 1), (1, 1), (0, 0)) if section == 0 else ((1, 0), (1, 1), (0, 1), (0, 0))
    rows = grads[0].shape[0]

    def group_shapes(count):
        tail = (count, 2, SUB, ZPART)
        return [jax.ShapeDtypeStruct(shape, bf16) for shape in ((2,) + tail, tail, tail)]

    return pl.pallas_call(
        functools.partial(weight_grad_kernel, order),
        out_shape=[jax.ShapeDtypeStruct((4, 2, SUB, XPART), bf16)] * Z
        + group_shapes(len(DISTANT))
        + group_shapes(len(CLOSE)),
        compiler_params=pltpu.CompilerParams(vmem_limit_bytes=40 * MIB),
        cost_estimate=pl.CostEstimate(
            flops=4 * rows * CHUNKS * WIDTH * COLS,
            bytes_accessed=4 * WIDTH * COLS,
            transcendentals=0,
        ),
    )(*grads, *codes, *gated, *hidden)


def to_local(value, pair, z_index):
    lead = value.shape[:-1]
    value = value.reshape(lead + (2, Z, SUB))
    axis = len(lead)
    value = jnp.where(pair == 0, value, jnp.flip(value, axis))
    doubled = jnp.concatenate([value, value], axis=axis + 1)
    return lax.dynamic_slice_in_dim(doubled, z_index, Z, axis + 1).reshape(lead + (WIDTH,))


def to_global(value, pair, z_index):
    return to_local(value, pair, (Z - z_index) % Z)


def on_device(codes_in, lengths, dec_weight, enc_weight, head):
    pipe = lax.axis_index("pipe")
    core, stage = pipe % 2, pipe // 2
    tensor = lax.axis_index("tensor")
    dp = lax.axis_index("dp")
    pair, z_index = dp // Z, dp % Z

    weights = gather_weights(dec_weight, enc_weight, core)

    codes_in = lax.dynamic_slice_in_dim(codes_in, tensor * CHUNKS, CHUNKS, 0)
    lengths = lax.dynamic_slice_in_dim(lengths, tensor * CHUNKS, CHUNKS, 0)
    codes_in = to_local(codes_in, pair, z_index)
    codes_in = jnp.where(stage == 0, codes_in, jnp.zeros_like(codes_in))
    head = to_local(head[None], pair, z_index)
    is_last = (stage == STAGES - 1).astype(jnp.int32)[None]

    rows = codes_in.shape[1]
    blank = jnp.zeros((rows, WIDTH), bf16)
    chunks = range(CHUNKS)
    received = [blank] * CHUNKS
    codes = [[None, None] for _ in chunks]
    gated = [[None, None] for _ in chunks]
    slope = [[None, None] for _ in chunks]
    seeds = [None] * CHUNKS
    for step in range(STAGES):
        keep = step == STAGES - 1
        for m in chunks:
            first = section_forward([received[m], codes_in[m]], weights[0], keep)
            second = section_forward([first[0], first[1], core_swap(first[1])], weights[1], keep)
            across = core_swap(second[1])
            if keep:
                codes[m] = [first[0], second[0]]
                gated[m] = [first[2], second[2]]
                slope[m] = [first[3], second[3]]
                seeds[m] = reward_seed(is_last, lengths[m], second[0], second[1], across, head)
            else:
                received[m] = y_shift(add(second[0], add(second[1], across)).astype(bf16), 1)

    received = [blank] * CHUNKS
    grads = [[None] * CHUNKS, [None] * CHUNKS]
    hidden = [[None] * CHUNKS, [None] * CHUNKS]
    through = [[None] * CHUNKS, [None] * CHUNKS]
    for step in range(STAGES):
        keep = step == STAGES - 1
        for m in chunks:
            second = section_backward([received[m], seeds[m]], slope[m][1], weights[1], keep)
            second_across = core_swap(second[1])
            first = section_backward(
                [second[0], codes[m][1], second[1], second_across], slope[m][0], weights[0], keep
            )
            first_across = core_swap(first[1])
            passed = norm_grad(
                first[0], codes[m][0], first[1], first_across, f32 if keep else bf16
            )
            if keep:
                grads[0][m], grads[1][m] = first[0], second[0]
                hidden[0][m], hidden[1][m] = first[2], second[2]
                through[0][m], through[1][m] = passed, first[3]
            else:
                received[m] = y_shift(passed, -1)

    parts = [None, None]
    for section in (1, 0):
        parts[section] = weight_grads(
            section,
            grads[section],
            [codes[m][section] for m in chunks],
            [gated[m][section] for m in chunks],
            hidden[section],
        )

    code_grads = jnp.where(core == 0, jnp.stack(through[0]), jnp.stack(through[1]))
    code_grads = to_global(code_grads, pair, z_index)
    share = rows // 2
    kept = lax.dynamic_slice_in_dim(code_grads, tensor * share, share, 1)
    sent = lax.dynamic_slice_in_dim(code_grads, (1 - tensor) * share, share, 1).astype(bf16)

    def code_exchange(others):
        (late,) = couple((sent,), others)
        return lax.ppermute(late, "tensor", [(0, 1), (1, 0)])

    sums, got = reduce_weights(parts, code_exchange)
    got = got.astype(f32)
    code_out = jnp.where(
        tensor == 0, jnp.concatenate([kept, got], axis=0), jnp.concatenate([got, kept], axis=0)
    )

    mine = jnp.where(core == 0, sums[0], sums[1])
    other = core_swap(jnp.where(core == 0, sums[1], sums[0]))
    full = jnp.where(
        core == 0,
        jnp.concatenate([mine, other], axis=-1),
        jnp.concatenate([other, mine], axis=-1),
    )
    return (code_out[None], full[0][None], full[1][None])


def solution(mesh):
    in_specs = (
        P(None, "dp", None),
        P(None, "dp"),
        P("pipe", "dp", "tensor"),
        P("pipe", "dp", "tensor"),
        P(),
    )
    out_specs = (
        P("pipe", None, ("dp", "tensor"), None),
        P("pipe", "dp", "tensor"),
        P("pipe", "dp", "tensor"),
    )
    return jax.shard_map(
        on_device, mesh=mesh, in_specs=in_specs, out_specs=out_specs, check_vma=False
    )
```

```python
import functools

import jax
import jax.numpy as jnp
from jax import lax
from jax.experimental import pallas as pl
from jax.experimental.pallas import tpu as pltpu
from jax.sharding import PartitionSpec as P

eps = 1e-05
loss_scale = 512.0
f32 = jnp.float32
bf16 = jnp.bfloat16

Z = 8
SUB = 32
WIDTH = 512
SPAN = 2048
COLS = 4096
XPART = 896
ZPART = SPAN - XPART
TILE = 1024
NEAR = (0, 1, 2, 6, 7)
FAR = (3, 4, 5)
RING = (0, 1, 2, 3, 5, 6, 7)
MIB = 1024 * 1024
CHUNKS = 1
MICROS = 2
STAGES = 4


def core_swap(value):
    return lax.ppermute(value, "pipe", [(i, i ^ 1) for i in range(8)])


def y_shift(value, steps):
    return lax.ppermute(
        value, "pipe", [(i, i + 2 * steps) for i in range(8) if 0 <= i + 2 * steps < 8]
    )


def z_shift(value, steps):
    return lax.ppermute(
        value, "dp", [(x * Z + z, x * Z + (z + steps) % Z) for x in range(2) for z in range(Z)]
    )


def swap_a(value):
    return lax.ppermute(value, "dp", [(x * Z + z, (1 - x) * Z + z) for x in range(2) for z in range(Z)])


def swap_b(value):
    pairs = [
        ((x * Z + z) * 2 + t, ((1 - x) * Z + z) * 2 + 1 - t)
        for x in range(2)
        for z in range(Z)
        for t in range(2)
    ]
    return lax.ppermute(value, ("dp", "tensor"), pairs)


def fenced(*values):
    return lax.optimization_barrier(values)


def copy_kernel(moves, n_in, *refs):
    sources, targets, sems = refs[:n_in], refs[n_in : n_in + 2], refs[n_in + 2]
    copies = []
    for k, (which, src, section, dst) in enumerate(moves):
        copy = pltpu.make_async_copy(
            sources[which].at[src], targets[section].at[dst], sems.at[k]
        )
        copy.start()
        copies.append(copy)
    for copy in copies:
        copy.wait()


def place(pieces, moves):
    vmem, hbm = pl.BlockSpec(memory_space=pltpu.VMEM), pl.BlockSpec(memory_space=pltpu.HBM)
    return pl.pallas_call(
        functools.partial(copy_kernel, moves, len(pieces)),
        out_shape=[jax.ShapeDtypeStruct((2, WIDTH, COLS), bf16)] * 2,
        in_specs=[hbm] * len(pieces),
        out_specs=[vmem, vmem],
        scratch_shapes=[pltpu.SemaphoreType.DMA((len(moves),))],
        compiler_params=pltpu.CompilerParams(vmem_limit_bytes=18 * MIB),
    )(*pieces)


def spot(xr, dz, tr, low, high):
    row = (xr * Z + dz) * SUB
    return (slice(None), slice(row, row + SUB), slice(tr * SPAN + low, tr * SPAN + high))


def narrow_moves(group, blocks, pieces, moves):
    for section in range(2):
        for (tr, xr), block in zip(((0, 0), (0, 1), (1, 1), (1, 0)), blocks[section]):
            for k, dz in enumerate(group):
                moves.append((len(pieces), (k,), section, spot(xr, dz, tr, XPART, SPAN)))
            pieces.append(block)


def ring_moves(dz, halves, pieces, moves):
    for section in range(2):
        for tr in range(2):
            for xr in range(2):
                which, index = (tr, 0) if len(halves) == 2 else (0, tr)
                moves.append(
                    (
                        len(pieces) + which,
                        (index, xr, section),
                        section,
                        spot(xr, dz, tr, 0, XPART),
                    )
                )
    pieces.extend(halves)


def gather_weights(dec_weight, enc_weight, core):
    own = jnp.stack([dec_weight[0], enc_weight[0]])
    mine = lax.dynamic_slice_in_dim(own, core * SPAN, SPAN, 2)
    other = core_swap(lax.dynamic_slice_in_dim(own, (1 - core) * SPAN, SPAN, 2))
    first = core == 0
    block = jnp.stack([jnp.where(first, mine, other), jnp.where(first, other, mine)])
    part_x, part_z = block[..., :XPART], block[..., XPART:]

    a, b, u1, d1 = fenced(
        swap_a(part_x), swap_b(part_x), z_shift(part_z, 1), z_shift(part_z, -1)
    )
    da, db, u2, d2 = fenced(swap_a(b[:1]), swap_b(a[1:]), z_shift(u1, 1), z_shift(d1, -1))
    ring = jnp.stack(
        [jnp.stack([part_x, a]), jnp.stack([jnp.concatenate([da, db], axis=0), b])]
    )
    near = [jnp.stack([t[s] for t in (part_z, d1, d2, u2, u1)]) for s in range(2)]
    w1, v1, near_a1, near_b0, u3, d3, near_a0, near_b1 = fenced(
        z_shift(ring, 1),
        z_shift(ring, -1),
        swap_a(near[1]),
        swap_b(near[0]),
        z_shift(u2, 1),
        z_shift(d2, -1),
        swap_a(near[0]),
        swap_b(near[1]),
    )
    w2, v2, near_d0, near_d1, u4, d4 = fenced(
        z_shift(w1, 1),
        z_shift(v1, -1),
        swap_a(near_b0),
        swap_b(near_a1),
        z_shift(u3[:1], 1),
        z_shift(d3[1:], -1),
    )
    far = [jnp.stack([d3[0], u4[0], u3[0]]), jnp.stack([d3[1], d4[0], u3[1]])]
    w3, v3, far_a1, far_b0, far_a0, far_b1 = fenced(
        z_shift(w2, 1),
        z_shift(v2, -1),
        swap_a(far[1]),
        swap_b(far[0]),
        swap_a(far[0]),
        swap_b(far[1]),
    )
    w4, v4 = z_shift(w3[:1], 1), z_shift(v3[1:], -1)
    far_d0, far_d1 = swap_a(far_b0), swap_b(far_a1)

    pieces, moves = [], []
    narrow_moves(
        NEAR,
        ((near[0], near_a0, near_b0, near_d0), (near[1], near_a1, near_b1, near_d1)),
        pieces,
        moves,
    )
    for dz, piece in ((0, ring), (1, v1), (7, w1), (2, v2), (6, w2)):
        ring_moves(dz, [piece], pieces, moves)
    narrow_moves(
        FAR,
        ((far[0], far_a0, far_b0, far_d0), (far[1], far_a1, far_b1, far_d1)),
        pieces,
        moves,
    )
    ring_moves(3, [v3], pieces, moves)
    ring_moves(5, [w3], pieces, moves)
    ring_moves(4, [w4, v4], pieces, moves)
    return place(pieces, moves)


def add(*terms):
    return functools.reduce(lambda a, b: a + b, [t.astype(f32) for t in terms])


def add_low(whole, part, axis):
    low, high = jnp.split(whole, 2, axis)
    return jnp.concatenate([add(low, part).astype(bf16), high], axis=axis)


def add_high(whole, part, axis):
    low, high = jnp.split(whole, 2, axis)
    return jnp.concatenate([low, add(high, part).astype(bf16)], axis=axis)


def couple(results, others):
    return lax.optimization_barrier((tuple(results), tuple(others)))[0]


def reduce_weights(ring, near, far, corners, code_exchange):
    (ring_40, near_0, far_0), (ring_41, near_1, far_1) = corners
    ring = {dz: ring[k] for k, dz in enumerate(RING)}
    z_res = (z_shift(ring_40, 1), z_shift(ring_41, -1))
    x_res = (swap_a(far_0[0]), swap_b(far_1[0]))
    z_send = (add_low(ring[3], z_res[0][:, :, None], 2), add_high(ring[5], z_res[1][:, :, None], 2))
    x_res = couple(x_res, z_send)
    x_send = (
        add_high(far[0, 1], x_res[1][:, None], 1),
        add_low(far[1, 1], x_res[0][:, None], 1),
    )
    z_res = couple((z_shift(z_send[0], 1), z_shift(z_send[1], -1)), x_send)
    x_res = (swap_a(x_send[0]), swap_b(x_send[1]))
    z_send = (add(ring[2], z_res[0]).astype(bf16), add(ring[6], z_res[1]).astype(bf16))
    x_res = couple(x_res, z_send)
    far_sum = add(far[0, 0], *x_res).astype(bf16)
    x_send = couple((near_0[0], near_1[0]), (far_sum,))
    z_res = couple((z_shift(z_send[0], 1), z_shift(z_send[1], -1)), x_send)
    n_res = (z_shift(far_sum[1, :1], 1), z_shift(far_sum[1, 1:], -1))
    x_res = (swap_a(x_send[0]), swap_b(x_send[1]))
    z_send = (add(ring[1], z_res[0]).astype(bf16), add(ring[7], z_res[1]).astype(bf16))
    n_send = (add_low(far_sum[0], n_res[0], 0), add_high(far_sum[2], n_res[1], 0))
    x_res = couple(x_res, z_send + n_send)
    x_send = (
        add_high(near[0, 1], x_res[1][:, None], 1),
        add_low(near[1, 1], x_res[0][:, None], 1),
    )
    z_res = couple((z_shift(z_send[0], 1), z_shift(z_send[1], -1)), x_send)
    n_res = couple((z_shift(n_send[0], 1), z_shift(n_send[1], -1)), x_send)
    x_res = (swap_a(x_send[0]), swap_b(x_send[1]))
    ring_sum = add(ring[0], *z_res).astype(bf16)
    x_res = couple(x_res, (ring_sum,))
    near_sum = add(near[0, 0], *x_res).astype(bf16)
    n_send = (add(near_sum[2], n_res[0]).astype(bf16), add(near_sum[3], n_res[1]).astype(bf16))
    n_res = (z_shift(n_send[0], 1), z_shift(n_send[1], -1))
    x_res = (swap_a(ring_sum[1, 0, :1]), swap_b(ring_sum[1, 0, 1:]))
    got = code_exchange(n_send)
    x_send = (add_high(ring_sum[0, 1], x_res[1], 0), add_low(ring_sum[1, 1], x_res[0], 0))
    n_res = couple(n_res, x_send)
    n_send = (add(near_sum[1], n_res[0]).astype(bf16), add(near_sum[4], n_res[1]).astype(bf16))
    x_res = (swap_a(x_send[0]), swap_b(x_send[1]))
    n_res = (z_shift(n_send[0], 1), z_shift(n_send[1], -1))
    return (
        jnp.concatenate([add(ring_sum[0, 0], *x_res), add(near_sum[0], *n_res)], axis=-1),
        got,
    )


def norm_of(codes):
    values = codes.astype(f32)
    scales = lax.rsqrt(jnp.mean(values * values, axis=-1, keepdims=True) + eps)
    return values, scales


def grad_through_norm(grad_out, codes, left, right):
    values, scales = norm_of(codes)
    summed = left.astype(f32) + right.astype(f32)
    inner = jnp.mean(summed * values, axis=-1, keepdims=True)
    return (
        grad_out.astype(f32) + scales * summed - values * (scales * scales * scales) * inner
    )


def dot_rows(left, right):
    return lax.dot_general(left, right, (((1,), (0,)), ((), ())), preferred_element_type=f32)


def dot_last(left, right):
    return lax.dot_general(left, right, (((1,), (1,)), ((), ())), preferred_element_type=f32)


def dot_first(left, right):
    return lax.dot_general(left, right, (((0,), (0,)), ((), ())), preferred_element_type=f32)


def forward_kernel(n_terms, keep, *refs):
    terms, weight_ref, outs = refs[:n_terms], refs[n_terms], refs[n_terms + 1 :]
    code_ref, part_ref = outs[:2]
    codes = terms[1][...].astype(f32)
    if n_terms == 3:
        codes = codes + terms[2][...].astype(f32)
    codes = (terms[0][...].astype(f32) + codes).astype(bf16)
    code_ref[...] = codes
    values, scales = norm_of(codes)
    normed = (values * scales).astype(bf16)
    total = None
    for low in range(0, COLS, TILE):
        span = slice(low, low + TILE)
        half = 0.5 * dot_rows(normed, weight_ref[0, :, span])
        bend = jnp.tanh(half)
        gated = (half + half * bend).astype(bf16)
        if keep:
            outs[2][:, span] = gated
            outs[3][:, span] = (0.5 * (1.0 + bend) * (1.0 + half * (1.0 - bend))).astype(bf16)
        part = dot_last(gated, weight_ref[1, :, span])
        total = part if total is None else total + part
    part_ref[...] = total.astype(bf16)


def section_cost(rows):
    return pl.CostEstimate(
        flops=4 * rows * WIDTH * COLS,
        bytes_accessed=4 * WIDTH * COLS + 8 * rows * WIDTH,
        transcendentals=rows * COLS,
    )


def section_forward(terms, weights, keep):
    rows = terms[0].shape[0]
    out_shape = [jax.ShapeDtypeStruct((rows, WIDTH), bf16)] * 2
    if keep:
        out_shape += [jax.ShapeDtypeStruct((rows, COLS), bf16)] * 2
    return pl.pallas_call(
        functools.partial(forward_kernel, len(terms), keep),
        out_shape=out_shape,
        compiler_params=pltpu.CompilerParams(vmem_limit_bytes=16 * MIB),
        cost_estimate=section_cost(rows),
    )(*terms, weights)


def backward_kernel(n_terms, keep, *refs):
    terms, slope_ref, weight_ref = refs[:n_terms], refs[n_terms], refs[n_terms + 1]
    outs = refs[n_terms + 2 :]
    grad_ref, part_ref = outs[:2]
    if n_terms == 2:
        grad = terms[0][...].astype(f32) + terms[1][...].astype(f32)
    else:
        grad = grad_through_norm(*[t[...] for t in terms])
        if keep:
            outs[3][...] = grad
    grad = grad.astype(bf16)
    grad_ref[...] = grad
    total = None
    for low in range(0, COLS, TILE):
        span = slice(low, low + TILE)
        gated_grad = dot_rows(grad, weight_ref[1, :, span])
        hidden_grad = (gated_grad * slope_ref[:, span].astype(f32)).astype(bf16)
        if keep:
            outs[2][:, span] = hidden_grad
        part = dot_last(hidden_grad, weight_ref[0, :, span])
        total = part if total is None else total + part
    part_ref[...] = total.astype(bf16)


def section_backward(terms, slope, weights, keep):
    rows = terms[0].shape[0]
    out_shape = [jax.ShapeDtypeStruct((rows, WIDTH), bf16)] * 2
    if keep:
        out_shape += [jax.ShapeDtypeStruct((rows, COLS), bf16)]
        if len(terms) > 2:
            out_shape += [jax.ShapeDtypeStruct((rows, WIDTH), f32)]
    return pl.pallas_call(
        functools.partial(backward_kernel, len(terms), keep),
        out_shape=out_shape,
        compiler_params=pltpu.CompilerParams(vmem_limit_bytes=16 * MIB),
        cost_estimate=section_cost(rows),
    )(*terms, slope, weights)


def norm_grad_kernel(grad_ref, code_ref, left_ref, right_ref, out_ref):
    out_ref[...] = grad_through_norm(
        grad_ref[...], code_ref[...], left_ref[...], right_ref[...]
    ).astype(out_ref.dtype)


def norm_grad(grad, codes, left, right, dtype):
    return pl.pallas_call(
        norm_grad_kernel, out_shape=jax.ShapeDtypeStruct(grad.shape, dtype)
    )(grad, codes, left, right)


def seed_kernel(flag_ref, lengths_ref, code_ref, left_ref, right_ref, head_ref, out_ref):
    codes = (
        code_ref[...].astype(f32) + (left_ref[...].astype(f32) + right_ref[...].astype(f32))
    ).astype(bf16)
    head = head_ref[...].astype(f32)
    all_scores = jnp.sum(codes.astype(f32) * head, axis=-1, keepdims=True)
    flag = jnp.full((1, 1), flag_ref[0], jnp.int32).astype(f32)
    rows = all_scores.shape[0] // MICROS
    seq_len = rows // 2
    for micro in range(MICROS):
        scores = all_scores[micro * rows : (micro + 1) * rows]
        position = lax.broadcasted_iota(jnp.int32, (rows, 1), 0)
        chosen_length, other_length = lengths_ref[micro, 0], lengths_ref[micro, 1]
        chosen = jnp.where(position < seq_len, 1.0, 0.0)
        limit = jnp.where(position < seq_len, chosen_length, other_length + seq_len)
        valid = jnp.where(position < limit, 1.0, 0.0)
        chosen_count = jnp.full((1, 1), chosen_length, jnp.int32).astype(f32)
        other_count = jnp.full((1, 1), other_length, jnp.int32).astype(f32)
        chosen_sum = jnp.sum(scores * valid * chosen, axis=0, keepdims=True)
        other_sum = jnp.sum(scores * valid * (1.0 - chosen), axis=0, keepdims=True)
        gap = other_sum / other_count - chosen_sum / chosen_count
        weight = loss_scale * jax.nn.sigmoid(gap)
        token = (1.0 - chosen) * (weight / other_count) - chosen * (weight / chosen_count)
        token = token * valid * flag
        out_ref[micro * rows : (micro + 1) * rows, :] = (token * head).astype(bf16)


def reward_seed(flag, lengths, codes, left, right, head):
    vmem = pl.BlockSpec(memory_space=pltpu.VMEM)
    smem = pl.BlockSpec(memory_space=pltpu.SMEM)
    return pl.pallas_call(
        seed_kernel,
        in_specs=[smem, smem, vmem, vmem, vmem, vmem],
        out_specs=vmem,
        out_shape=jax.ShapeDtypeStruct(codes.shape, bf16),
    )(flag, lengths, codes, left, right, head)


def weight_grad_kernel(*refs):
    grads, codes = refs[0:CHUNKS], refs[CHUNKS : 2 * CHUNKS]
    gated, hidden = refs[2 * CHUNKS : 3 * CHUNKS], refs[3 * CHUNKS : 4 * CHUNKS]
    ring_ref, near_ref, far_ref, ring_4, near_corner, far_corner = refs[-6:]

    def joined(group):
        return jnp.concatenate([ref[...] for ref in group], axis=0)

    values, scales = norm_of(joined(codes))
    normed = (values * scales).astype(bf16)
    for mat, (left, group) in enumerate(((normed, hidden), (joined(grads), gated))):
        for low, high in ((0, XPART), (XPART, SPAN)):
            right = jnp.concatenate([ref[:, low:high] for ref in group], axis=0)
            result = dot_first(left, right).astype(bf16)
            for xr in range(2):
                for dz in range(Z):
                    row = (xr * Z + dz) * SUB
                    piece = result[row : row + SUB]
                    if low == 0 and dz == 4:
                        ring_4[0, xr, mat] = piece
                    elif low == 0:
                        ring_ref[RING.index(dz), 0, xr, 0, mat] = piece
                    elif dz in NEAR:
                        k = NEAR.index(dz)
                        near_ref[0, xr, k, 0, mat] = piece
                        if xr == 0:
                            near_corner[0, k, mat] = piece
                    else:
                        k = FAR.index(dz)
                        far_ref[0, xr, k, 0, mat] = piece
                        if xr == 0:
                            far_corner[0, k, mat] = piece


def weight_grads(section, grads, codes, gated, hidden, held):
    rows = grads[0].shape[0]
    narrow = pl.BlockSpec((rows, WIDTH), lambda t: (0, 0))
    wide = pl.BlockSpec((rows, SPAN), lambda t: (0, t))
    n_in = 4 * CHUNKS

    def group_spec(count):
        return pl.BlockSpec(
            (1, 2, count, 1, 2, SUB, ZPART), lambda t: (t, 0, 0, section, 0, 0, 0)
        )

    def corner_spec(count):
        return pl.BlockSpec((1, count, 2, SUB, ZPART), lambda t: (0, 0, 0, 0, 0))

    return pl.pallas_call(
        weight_grad_kernel,
        grid=(2,),
        in_specs=[narrow] * (2 * CHUNKS)
        + [wide] * (2 * CHUNKS)
        + [pl.BlockSpec(memory_space=pl.ANY)] * len(held),
        out_specs=[
            pl.BlockSpec(
                (len(RING), 1, 2, 1, 2, SUB, XPART), lambda t: (0, t, 0, section, 0, 0, 0)
            ),
            group_spec(len(NEAR)),
            group_spec(len(FAR)),
            pl.BlockSpec((1, 2, 2, SUB, XPART), lambda t: (t, 0, 0, 0, 0)),
            corner_spec(len(NEAR)),
            corner_spec(len(FAR)),
        ],
        out_shape=[
            jax.ShapeDtypeStruct((len(RING), 2, 2, 2, 2, SUB, XPART), bf16),
            jax.ShapeDtypeStruct((2, 2, len(NEAR), 2, 2, SUB, ZPART), bf16),
            jax.ShapeDtypeStruct((2, 2, len(FAR), 2, 2, SUB, ZPART), bf16),
            jax.ShapeDtypeStruct((2, 2, 2, SUB, XPART), bf16),
            jax.ShapeDtypeStruct((1, len(NEAR), 2, SUB, ZPART), bf16),
            jax.ShapeDtypeStruct((1, len(FAR), 2, SUB, ZPART), bf16),
        ],
        input_output_aliases={n_in + k: k for k in range(len(held))},
        compiler_params=pltpu.CompilerParams(vmem_limit_bytes=30 * MIB),
        cost_estimate=pl.CostEstimate(
            flops=8 * rows * CHUNKS * WIDTH * COLS // 2,
            bytes_accessed=4 * WIDTH * COLS,
            transcendentals=0,
        ),
    )(*grads, *codes, *gated, *hidden, *held)


def to_local(value, pair, z_index):
    lead = value.shape[:-1]
    value = value.reshape(lead + (2, Z, SUB))
    axis = len(lead)
    value = jnp.where(pair == 0, value, jnp.flip(value, axis))
    doubled = jnp.concatenate([value, value], axis=axis + 1)
    return lax.dynamic_slice_in_dim(doubled, z_index, Z, axis + 1).reshape(lead + (WIDTH,))


def to_global(value, pair, z_index):
    return to_local(value, pair, (Z - z_index) % Z)


def on_device(codes_in, lengths, dec_weight, enc_weight, head):
    pipe = lax.axis_index("pipe")
    core, stage = pipe % 2, pipe // 2
    tensor = lax.axis_index("tensor")
    dp = lax.axis_index("dp")
    pair, z_index = dp // Z, dp % Z

    weights = gather_weights(dec_weight, enc_weight, core)

    codes_in = lax.dynamic_slice_in_dim(codes_in, tensor * MICROS, MICROS, 0)
    lengths = lax.dynamic_slice_in_dim(lengths, tensor * MICROS, MICROS, 0)
    lengths = lengths.reshape(CHUNKS, MICROS // CHUNKS, 2)
    codes_in = to_local(codes_in, pair, z_index).reshape(CHUNKS, -1, WIDTH)
    codes_in = jnp.where(stage == 0, codes_in, jnp.zeros_like(codes_in))
    head = to_local(head[None], pair, z_index)
    is_last = (stage == STAGES - 1).astype(jnp.int32)[None]

    rows = codes_in.shape[1]
    blank = jnp.zeros((rows, WIDTH), bf16)
    chunks = range(CHUNKS)
    received = [blank] * CHUNKS
    codes = [[None, None] for _ in chunks]
    gated = [[None, None] for _ in chunks]
    slope = [[None, None] for _ in chunks]
    seeds = [None] * CHUNKS
    for step in range(STAGES):
        keep = step == STAGES - 1
        for m in chunks:
            first = section_forward([received[m], codes_in[m]], weights[0], keep)
            second = section_forward([first[0], first[1], core_swap(first[1])], weights[1], keep)
            across = core_swap(second[1])
            if keep:
                codes[m] = [first[0], second[0]]
                gated[m] = [first[2], second[2]]
                slope[m] = [first[3], second[3]]
                seeds[m] = reward_seed(is_last, lengths[m], second[0], second[1], across, head)
            else:
                received[m] = y_shift(add(second[0], add(second[1], across)).astype(bf16), 1)

    received = [blank] * CHUNKS
    grads = [[None] * CHUNKS, [None] * CHUNKS]
    hidden = [[None] * CHUNKS, [None] * CHUNKS]
    through = [[None] * CHUNKS, [None] * CHUNKS]
    for step in range(STAGES):
        keep = step == STAGES - 1
        for m in chunks:
            second = section_backward([received[m], seeds[m]], slope[m][1], weights[1], keep)
            second_across = core_swap(second[1])
            first = section_backward(
                [second[0], codes[m][1], second[1], second_across], slope[m][0], weights[0], keep
            )
            first_across = core_swap(first[1])
            passed = norm_grad(
                first[0], codes[m][0], first[1], first_across, f32 if keep else bf16
            )
            if keep:
                grads[0][m], grads[1][m] = first[0], second[0]
                hidden[0][m], hidden[1][m] = first[2], second[2]
                through[0][m], through[1][m] = passed, first[3]
            else:
                received[m] = y_shift(passed, -1)

    held, corners = (), [None, None]
    for section in (1, 0):
        made = weight_grads(
            section,
            grads[section],
            [codes[m][section] for m in chunks],
            [gated[m][section] for m in chunks],
            hidden[section],
            held,
        )
        held, corners[section] = made[:3], made[3:]

    code_grads = jnp.where(core == 0, jnp.stack(through[0]), jnp.stack(through[1]))
    code_grads = to_global(code_grads.reshape(MICROS, -1, WIDTH), pair, z_index)
    share = code_grads.shape[1] // 2
    kept = lax.dynamic_slice_in_dim(code_grads, tensor * share, share, 1)
    sent = lax.dynamic_slice_in_dim(code_grads, (1 - tensor) * share, share, 1).astype(bf16)

    def code_exchange(others):
        (late,) = couple((sent,), others)
        return lax.ppermute(late, "tensor", [(0, 1), (1, 0)])

    summed, got = reduce_weights(*held, corners, code_exchange)
    got = got.astype(f32)
    code_out = jnp.where(
        tensor == 0, jnp.concatenate([kept, got], axis=0), jnp.concatenate([got, kept], axis=0)
    )

    mine = lax.dynamic_index_in_dim(summed, core, 0, keepdims=False)
    other = core_swap(lax.dynamic_index_in_dim(summed, 1 - core, 0, keepdims=False))
    full = jnp.where(
        core == 0,
        jnp.concatenate([mine, other], axis=-1),
        jnp.concatenate([other, mine], axis=-1),
    )
    return (code_out[None], full[0][None], full[1][None])


def solution(mesh):
    in_specs = (
        P(None, "dp", None),
        P(None, "dp"),
        P("pipe", "dp", "tensor"),
        P("pipe", "dp", "tensor"),
        P(),
    )
    out_specs = (
        P("pipe", None, ("dp", "tensor"), None),
        P("pipe", "dp", "tensor"),
        P("pipe", "dp", "tensor"),
    )
    return jax.shard_map(
        on_device, mesh=mesh, in_specs=in_specs, out_specs=out_specs, check_vma=False
    )
```

```python
import functools

import jax
import jax.numpy as jnp
from jax import lax
from jax.experimental import pallas as pl
from jax.experimental.pallas import tpu as pltpu
from jax.sharding import PartitionSpec as P

eps = 1e-05
loss_scale = 512.0
f32 = jnp.float32
bf16 = jnp.bfloat16

Z = 8
SUB = 32
WIDTH = 512
SPAN = 2048
COLS = 4096
XPART = 896
ZPART = SPAN - XPART
TILE = 1024
NEAR = (0, 1, 2, 6, 7)
FAR = (3, 4, 5)
MIB = 1024 * 1024
CHUNKS = 1
MICROS = 2
STAGES = 4


def core_swap(value):
    return lax.ppermute(value, "pipe", [(i, i ^ 1) for i in range(8)])


def y_shift(value, steps):
    return lax.ppermute(
        value, "pipe", [(i, i + 2 * steps) for i in range(8) if 0 <= i + 2 * steps < 8]
    )


def z_shift(value, steps):
    return lax.ppermute(
        value, "dp", [(x * Z + z, x * Z + (z + steps) % Z) for x in range(2) for z in range(Z)]
    )


def swap_a(value):
    return lax.ppermute(value, "dp", [(x * Z + z, (1 - x) * Z + z) for x in range(2) for z in range(Z)])


def swap_b(value):
    pairs = [
        ((x * Z + z) * 2 + t, ((1 - x) * Z + z) * 2 + 1 - t)
        for x in range(2)
        for z in range(Z)
        for t in range(2)
    ]
    return lax.ppermute(value, ("dp", "tensor"), pairs)


def fenced(*values):
    return lax.optimization_barrier(values)


def copy_kernel(moves, n_in, *refs):
    z_ref, sources = refs[0], refs[1 : n_in + 1]
    targets, sems = refs[n_in + 1 : n_in + 3], refs[n_in + 3]
    copies = []
    for k, (which, src, section, dst) in enumerate(moves):
        rows, columns = dst
        if isinstance(rows, tuple):
            start, z = rows
            start = pl.multiple_of(start + lax.rem(z - z_ref[0] + Z, Z) * SUB, SUB)
            rows = pl.ds(start, SUB)
        copy = pltpu.make_async_copy(
            sources[which].at[src], targets[section].at[:, rows, columns], sems.at[k]
        )
        copy.start()
        copies.append(copy)
    for copy in copies:
        copy.wait()


def place(z_index, pieces, moves):
    vmem, hbm = pl.BlockSpec(memory_space=pltpu.VMEM), pl.BlockSpec(memory_space=pl.ANY)
    return pl.pallas_call(
        functools.partial(copy_kernel, moves, len(pieces)),
        out_shape=[jax.ShapeDtypeStruct((2, WIDTH, COLS), bf16)] * 2,
        in_specs=[pl.BlockSpec(memory_space=pltpu.SMEM)] + [hbm] * len(pieces),
        out_specs=[vmem, vmem],
        scratch_shapes=[pltpu.SemaphoreType.DMA((len(moves),))],
        compiler_params=pltpu.CompilerParams(vmem_limit_bytes=18 * MIB),
    )(z_index, *pieces)


def spot(xr, dz, tr, low, high):
    row = (xr * Z + dz) * SUB
    return (slice(row, row + SUB), slice(tr * SPAN + low, tr * SPAN + high))


def narrow_moves(group, blocks, pieces, moves):
    for section in range(2):
        for (tr, xr), block in zip(((0, 0), (0, 1), (1, 1), (1, 0)), blocks[section]):
            for k, dz in enumerate(group):
                moves.append((len(pieces), (k,), section, spot(xr, dz, tr, XPART, SPAN)))
            pieces.append(block)


def ring_moves(gathered, pieces, moves):
    for section in range(2):
        for z in range(Z):
            for tr in range(2):
                for xr in range(2):
                    columns = slice(tr * SPAN, tr * SPAN + XPART)
                    moves.append(
                        (len(pieces), (z, tr, xr, section), section, ((xr * Z * SUB, z), columns))
                    )
    pieces.append(gathered)


Z_GROUPS = [list(range(Z)), list(range(Z, 2 * Z))]


def gather_weights(dec_weight, enc_weight, core, z_index):
    own = jnp.stack([dec_weight[0], enc_weight[0]])
    mine = lax.dynamic_slice_in_dim(own, core * SPAN, SPAN, 2)
    other = core_swap(lax.dynamic_slice_in_dim(own, (1 - core) * SPAN, SPAN, 2))
    first = core == 0
    block = jnp.stack([jnp.where(first, mine, other), jnp.where(first, other, mine)])
    part_x, part_z = block[..., :XPART], block[..., XPART:]

    a, b, u1, d1 = fenced(
        swap_a(part_x), swap_b(part_x), z_shift(part_z, 1), z_shift(part_z, -1)
    )
    da, db, u2, d2 = fenced(swap_a(b[:1]), swap_b(a[1:]), z_shift(u1, 1), z_shift(d1, -1))
    ring = jnp.stack(
        [jnp.stack([part_x, a]), jnp.stack([jnp.concatenate([da, db], axis=0), b])]
    )
    gathered = lax.all_gather(ring, "dp", axis=0, axis_index_groups=Z_GROUPS)
    near = [jnp.stack([t[s] for t in (part_z, d1, d2, u2, u1)]) for s in range(2)]
    near_a1, near_b0, u3, d3, near_a0, near_b1 = fenced(
        swap_a(near[1]),
        swap_b(near[0]),
        z_shift(u2, 1),
        z_shift(d2, -1),
        swap_a(near[0]),
        swap_b(near[1]),
    )
    near_d0, near_d1, u4, d4 = fenced(
        swap_a(near_b0), swap_b(near_a1), z_shift(u3[:1], 1), z_shift(d3[1:], -1)
    )
    far = [jnp.stack([d3[0], u4[0], u3[0]]), jnp.stack([d3[1], d4[0], u3[1]])]
    far_a1, far_b0, far_a0, far_b1 = fenced(
        swap_a(far[1]), swap_b(far[0]), swap_a(far[0]), swap_b(far[1])
    )
    far_d0, far_d1 = swap_a(far_b0), swap_b(far_a1)

    pieces, moves = [], []
    narrow_moves(
        NEAR,
        ((near[0], near_a0, near_b0, near_d0), (near[1], near_a1, near_b1, near_d1)),
        pieces,
        moves,
    )
    narrow_moves(
        FAR,
        ((far[0], far_a0, far_b0, far_d0), (far[1], far_a1, far_b1, far_d1)),
        pieces,
        moves,
    )
    ring_moves(gathered, pieces, moves)
    return place(z_index, pieces, moves)


def add(*terms):
    return functools.reduce(lambda a, b: a + b, [t.astype(f32) for t in terms])


def add_low(whole, part, axis):
    low, high = jnp.split(whole, 2, axis)
    return jnp.concatenate([add(low, part).astype(bf16), high], axis=axis)


def add_high(whole, part, axis):
    low, high = jnp.split(whole, 2, axis)
    return jnp.concatenate([low, add(high, part).astype(bf16)], axis=axis)


def couple(results, others):
    return lax.optimization_barrier((tuple(results), tuple(others)))[0]


def reduce_weights(ring, near, far, corners, code_exchange):
    (near_0, far_0), (near_1, far_1) = corners
    ring_sum = lax.psum_scatter(
        ring, "dp", scatter_dimension=0, axis_index_groups=Z_GROUPS, tiled=True
    )[0]
    x_res = (swap_a(far_0[0]), swap_b(far_1[0]))
    x_send = (
        add_high(far[0, 1], x_res[1][:, None], 1),
        add_low(far[1, 1], x_res[0][:, None], 1),
    )
    x_res = (swap_a(x_send[0]), swap_b(x_send[1]))
    far_sum = add(far[0, 0], *x_res).astype(bf16)
    x_send = couple((near_0[0], near_1[0]), (far_sum,))
    n_res = (z_shift(far_sum[1, :1], 1), z_shift(far_sum[1, 1:], -1))
    x_res = (swap_a(x_send[0]), swap_b(x_send[1]))
    n_send = (add_low(far_sum[0], n_res[0], 0), add_high(far_sum[2], n_res[1], 0))
    x_res = couple(x_res, n_send)
    x_send = (
        add_high(near[0, 1], x_res[1][:, None], 1),
        add_low(near[1, 1], x_res[0][:, None], 1),
    )
    n_res = couple((z_shift(n_send[0], 1), z_shift(n_send[1], -1)), x_send)
    x_res = (swap_a(x_send[0]), swap_b(x_send[1]))
    near_sum = add(near[0, 0], *x_res).astype(bf16)
    n_send = (add(near_sum[2], n_res[0]).astype(bf16), add(near_sum[3], n_res[1]).astype(bf16))
    got = code_exchange(n_send)
    n_res = (z_shift(n_send[0], 1), z_shift(n_send[1], -1))
    x_res = (swap_a(ring_sum[1, 0, :1]), swap_b(ring_sum[1, 0, 1:]))
    x_send = (add_high(ring_sum[0, 1], x_res[1], 0), add_low(ring_sum[1, 1], x_res[0], 0))
    n_res = couple(n_res, x_send)
    x_send = couple(x_send, (got,))
    n_send = (add(near_sum[1], n_res[0]).astype(bf16), add(near_sum[4], n_res[1]).astype(bf16))
    x_res = (swap_a(x_send[0]), swap_b(x_send[1]))
    n_res = (z_shift(n_send[0], 1), z_shift(n_send[1], -1))
    return (
        jnp.concatenate([add(ring_sum[0, 0], *x_res), add(near_sum[0], *n_res)], axis=-1),
        got,
    )


def norm_of(codes):
    values = codes.astype(f32)
    scales = lax.rsqrt(jnp.mean(values * values, axis=-1, keepdims=True) + eps)
    return values, scales


def grad_through_norm(grad_out, codes, left, right):
    values, scales = norm_of(codes)
    summed = left.astype(f32) + right.astype(f32)
    inner = jnp.mean(summed * values, axis=-1, keepdims=True)
    return (
        grad_out.astype(f32) + scales * summed - values * (scales * scales * scales) * inner
    )


def dot_rows(left, right):
    return lax.dot_general(left, right, (((1,), (0,)), ((), ())), preferred_element_type=f32)


def dot_last(left, right):
    return lax.dot_general(left, right, (((1,), (1,)), ((), ())), preferred_element_type=f32)


def dot_first(left, right):
    return lax.dot_general(left, right, (((0,), (0,)), ((), ())), preferred_element_type=f32)


def forward_kernel(n_terms, keep, *refs):
    terms, weight_ref, outs = refs[:n_terms], refs[n_terms], refs[n_terms + 1 :]
    code_ref, part_ref = outs[:2]
    codes = terms[1][...].astype(f32)
    if n_terms == 3:
        codes = codes + terms[2][...].astype(f32)
    codes = (terms[0][...].astype(f32) + codes).astype(bf16)
    code_ref[...] = codes
    values, scales = norm_of(codes)
    normed = (values * scales).astype(bf16)
    total = None
    for low in range(0, COLS, TILE):
        span = slice(low, low + TILE)
        half = 0.5 * dot_rows(normed, weight_ref[0, :, span])
        bend = jnp.tanh(half)
        gated = (half + half * bend).astype(bf16)
        if keep:
            outs[2][:, span] = gated
            outs[3][:, span] = (0.5 * (1.0 + bend) * (1.0 + half * (1.0 - bend))).astype(bf16)
        part = dot_last(gated, weight_ref[1, :, span])
        total = part if total is None else total + part
    part_ref[...] = total.astype(bf16)


def section_cost(rows):
    return pl.CostEstimate(
        flops=4 * rows * WIDTH * COLS,
        bytes_accessed=4 * WIDTH * COLS + 8 * rows * WIDTH,
        transcendentals=rows * COLS,
    )


def section_forward(terms, weights, keep):
    rows = terms[0].shape[0]
    out_shape = [jax.ShapeDtypeStruct((rows, WIDTH), bf16)] * 2
    if keep:
        out_shape += [jax.ShapeDtypeStruct((rows, COLS), bf16)] * 2
    return pl.pallas_call(
        functools.partial(forward_kernel, len(terms), keep),
        out_shape=out_shape,
        compiler_params=pltpu.CompilerParams(vmem_limit_bytes=16 * MIB),
        cost_estimate=section_cost(rows),
    )(*terms, weights)


def backward_kernel(n_terms, keep, *refs):
    terms, slope_ref, weight_ref = refs[:n_terms], refs[n_terms], refs[n_terms + 1]
    outs = refs[n_terms + 2 :]
    grad_ref, part_ref = outs[:2]
    if n_terms == 2:
        grad = terms[0][...].astype(f32) + terms[1][...].astype(f32)
    else:
        grad = grad_through_norm(*[t[...] for t in terms])
        if keep:
            outs[3][...] = grad
    grad = grad.astype(bf16)
    grad_ref[...] = grad
    total = None
    for low in range(0, COLS, TILE):
        span = slice(low, low + TILE)
        gated_grad = dot_rows(grad, weight_ref[1, :, span])
        hidden_grad = (gated_grad * slope_ref[:, span].astype(f32)).astype(bf16)
        if keep:
            outs[2][:, span] = hidden_grad
        part = dot_last(hidden_grad, weight_ref[0, :, span])
        total = part if total is None else total + part
    part_ref[...] = total.astype(bf16)


def section_backward(terms, slope, weights, keep):
    rows = terms[0].shape[0]
    out_shape = [jax.ShapeDtypeStruct((rows, WIDTH), bf16)] * 2
    if keep:
        out_shape += [jax.ShapeDtypeStruct((rows, COLS), bf16)]
        if len(terms) > 2:
            out_shape += [jax.ShapeDtypeStruct((rows, WIDTH), f32)]
    return pl.pallas_call(
        functools.partial(backward_kernel, len(terms), keep),
        out_shape=out_shape,
        compiler_params=pltpu.CompilerParams(vmem_limit_bytes=16 * MIB),
        cost_estimate=section_cost(rows),
    )(*terms, slope, weights)


def norm_grad_kernel(grad_ref, code_ref, left_ref, right_ref, out_ref):
    out_ref[...] = grad_through_norm(
        grad_ref[...], code_ref[...], left_ref[...], right_ref[...]
    ).astype(out_ref.dtype)


def norm_grad(grad, codes, left, right, dtype):
    return pl.pallas_call(
        norm_grad_kernel, out_shape=jax.ShapeDtypeStruct(grad.shape, dtype)
    )(grad, codes, left, right)


def seed_kernel(flag_ref, lengths_ref, code_ref, left_ref, right_ref, head_ref, out_ref):
    codes = (
        code_ref[...].astype(f32) + (left_ref[...].astype(f32) + right_ref[...].astype(f32))
    ).astype(bf16)
    head = head_ref[...].astype(f32)
    all_scores = jnp.sum(codes.astype(f32) * head, axis=-1, keepdims=True)
    flag = jnp.full((1, 1), flag_ref[0], jnp.int32).astype(f32)
    rows = all_scores.shape[0] // MICROS
    seq_len = rows // 2
    for micro in range(MICROS):
        scores = all_scores[micro * rows : (micro + 1) * rows]
        position = lax.broadcasted_iota(jnp.int32, (rows, 1), 0)
        chosen_length, other_length = lengths_ref[micro, 0], lengths_ref[micro, 1]
        chosen = jnp.where(position < seq_len, 1.0, 0.0)
        limit = jnp.where(position < seq_len, chosen_length, other_length + seq_len)
        valid = jnp.where(position < limit, 1.0, 0.0)
        chosen_count = jnp.full((1, 1), chosen_length, jnp.int32).astype(f32)
        other_count = jnp.full((1, 1), other_length, jnp.int32).astype(f32)
        chosen_sum = jnp.sum(scores * valid * chosen, axis=0, keepdims=True)
        other_sum = jnp.sum(scores * valid * (1.0 - chosen), axis=0, keepdims=True)
        gap = other_sum / other_count - chosen_sum / chosen_count
        weight = loss_scale * jax.nn.sigmoid(gap)
        token = (1.0 - chosen) * (weight / other_count) - chosen * (weight / chosen_count)
        token = token * valid * flag
        out_ref[micro * rows : (micro + 1) * rows, :] = (token * head).astype(bf16)


def reward_seed(flag, lengths, codes, left, right, head):
    vmem = pl.BlockSpec(memory_space=pltpu.VMEM)
    smem = pl.BlockSpec(memory_space=pltpu.SMEM)
    return pl.pallas_call(
        seed_kernel,
        in_specs=[smem, smem, vmem, vmem, vmem, vmem],
        out_specs=vmem,
        out_shape=jax.ShapeDtypeStruct(codes.shape, bf16),
    )(flag, lengths, codes, left, right, head)


def weight_grad_kernel(*refs):
    z_ref, refs = refs[0], refs[1:]
    grads, codes = refs[0:CHUNKS], refs[CHUNKS : 2 * CHUNKS]
    gated, hidden = refs[2 * CHUNKS : 3 * CHUNKS], refs[3 * CHUNKS : 4 * CHUNKS]
    ring_ref, near_ref, far_ref, near_corner, far_corner = refs[-5:]

    def joined(group):
        return jnp.concatenate([ref[...] for ref in group], axis=0)

    values, scales = norm_of(joined(codes))
    normed = (values * scales).astype(bf16)
    for mat, (left, group) in enumerate(((normed, hidden), (joined(grads), gated))):
        for low, high in ((0, XPART), (XPART, SPAN)):
            right = jnp.concatenate([ref[:, low:high] for ref in group], axis=0)
            result = dot_first(left, right).astype(bf16)
            for xr in range(2):
                for dz in range(Z):
                    row = (xr * Z + dz) * SUB
                    piece = result[row : row + SUB]
                    if low == 0:
                        ring_ref[lax.rem(z_ref[0] + dz, Z), 0, xr, 0, mat] = piece
                    elif dz in NEAR:
                        k = NEAR.index(dz)
                        near_ref[0, xr, k, 0, mat] = piece
                        if xr == 0:
                            near_corner[0, k, mat] = piece
                    else:
                        k = FAR.index(dz)
                        far_ref[0, xr, k, 0, mat] = piece
                        if xr == 0:
                            far_corner[0, k, mat] = piece


def weight_grads(section, z_index, grads, codes, gated, hidden, held):
    rows = grads[0].shape[0]
    narrow = pl.BlockSpec((rows, WIDTH), lambda t: (0, 0))
    wide = pl.BlockSpec((rows, SPAN), lambda t: (0, t))
    n_in = 4 * CHUNKS + 1

    def group_spec(count):
        return pl.BlockSpec(
            (1, 2, count, 1, 2, SUB, ZPART), lambda t: (t, 0, 0, section, 0, 0, 0)
        )

    def corner_spec(count):
        return pl.BlockSpec((1, count, 2, SUB, ZPART), lambda t: (0, 0, 0, 0, 0))

    return pl.pallas_call(
        weight_grad_kernel,
        grid=(2,),
        in_specs=[pl.BlockSpec(memory_space=pltpu.SMEM)]
        + [narrow] * (2 * CHUNKS)
        + [wide] * (2 * CHUNKS)
        + [pl.BlockSpec(memory_space=pl.ANY)] * len(held),
        out_specs=[
            pl.BlockSpec((Z, 1, 2, 1, 2, SUB, XPART), lambda t: (0, t, 0, section, 0, 0, 0)),
            group_spec(len(NEAR)),
            group_spec(len(FAR)),
            corner_spec(len(NEAR)),
            corner_spec(len(FAR)),
        ],
        out_shape=[
            jax.ShapeDtypeStruct((Z, 2, 2, 2, 2, SUB, XPART), bf16),
            jax.ShapeDtypeStruct((2, 2, len(NEAR), 2, 2, SUB, ZPART), bf16),
            jax.ShapeDtypeStruct((2, 2, len(FAR), 2, 2, SUB, ZPART), bf16),
            jax.ShapeDtypeStruct((1, len(NEAR), 2, SUB, ZPART), bf16),
            jax.ShapeDtypeStruct((1, len(FAR), 2, SUB, ZPART), bf16),
        ],
        input_output_aliases={n_in + k: k for k in range(len(held))},
        compiler_params=pltpu.CompilerParams(vmem_limit_bytes=30 * MIB),
        cost_estimate=pl.CostEstimate(
            flops=8 * rows * CHUNKS * WIDTH * COLS // 2,
            bytes_accessed=4 * WIDTH * COLS,
            transcendentals=0,
        ),
    )(z_index, *grads, *codes, *gated, *hidden, *held)


def to_local(value, pair, z_index):
    lead = value.shape[:-1]
    value = value.reshape(lead + (2, Z, SUB))
    axis = len(lead)
    value = jnp.where(pair == 0, value, jnp.flip(value, axis))
    doubled = jnp.concatenate([value, value], axis=axis + 1)
    return lax.dynamic_slice_in_dim(doubled, z_index, Z, axis + 1).reshape(lead + (WIDTH,))


def to_global(value, pair, z_index):
    return to_local(value, pair, (Z - z_index) % Z)


def on_device(codes_in, lengths, dec_weight, enc_weight, head):
    pipe = lax.axis_index("pipe")
    core, stage = pipe % 2, pipe // 2
    tensor = lax.axis_index("tensor")
    dp = lax.axis_index("dp")
    pair, z_index = dp // Z, dp % Z

    weights = gather_weights(dec_weight, enc_weight, core, z_index[None])

    codes_in = lax.dynamic_slice_in_dim(codes_in, tensor * MICROS, MICROS, 0)
    lengths = lax.dynamic_slice_in_dim(lengths, tensor * MICROS, MICROS, 0)
    lengths = lengths.reshape(CHUNKS, MICROS // CHUNKS, 2)
    codes_in = to_local(codes_in, pair, z_index).reshape(CHUNKS, -1, WIDTH)
    codes_in = jnp.where(stage == 0, codes_in, jnp.zeros_like(codes_in))
    head = to_local(head[None], pair, z_index)
    is_last = (stage == STAGES - 1).astype(jnp.int32)[None]

    rows = codes_in.shape[1]
    blank = jnp.zeros((rows, WIDTH), bf16)
    chunks = range(CHUNKS)
    received = [blank] * CHUNKS
    codes = [[None, None] for _ in chunks]
    gated = [[None, None] for _ in chunks]
    slope = [[None, None] for _ in chunks]
    seeds = [None] * CHUNKS
    for step in range(STAGES):
        keep = step == STAGES - 1
        for m in chunks:
            first = section_forward([received[m], codes_in[m]], weights[0], keep)
            second = section_forward([first[0], first[1], core_swap(first[1])], weights[1], keep)
            across = core_swap(second[1])
            if keep:
                codes[m] = [first[0], second[0]]
                gated[m] = [first[2], second[2]]
                slope[m] = [first[3], second[3]]
                seeds[m] = reward_seed(is_last, lengths[m], second[0], second[1], across, head)
            else:
                received[m] = y_shift(add(second[0], add(second[1], across)).astype(bf16), 1)

    received = [blank] * CHUNKS
    grads = [[None] * CHUNKS, [None] * CHUNKS]
    hidden = [[None] * CHUNKS, [None] * CHUNKS]
    through = [[None] * CHUNKS, [None] * CHUNKS]
    for step in range(STAGES):
        keep = step == STAGES - 1
        for m in chunks:
            second = section_backward([received[m], seeds[m]], slope[m][1], weights[1], keep)
            second_across = core_swap(second[1])
            first = section_backward(
                [second[0], codes[m][1], second[1], second_across], slope[m][0], weights[0], keep
            )
            first_across = core_swap(first[1])
            passed = norm_grad(
                first[0], codes[m][0], first[1], first_across, f32 if keep else bf16
            )
            if keep:
                grads[0][m], grads[1][m] = first[0], second[0]
                hidden[0][m], hidden[1][m] = first[2], second[2]
                through[0][m], through[1][m] = passed, first[3]
            else:
                received[m] = y_shift(passed, -1)

    held, corners = (), [None, None]
    for section in (1, 0):
        made = weight_grads(
            section,
            z_index[None],
            grads[section],
            [codes[m][section] for m in chunks],
            [gated[m][section] for m in chunks],
            hidden[section],
            held,
        )
        held, corners[section] = made[:3], made[3:]

    code_grads = jnp.where(core == 0, jnp.stack(through[0]), jnp.stack(through[1]))
    code_grads = to_global(code_grads.reshape(MICROS, -1, WIDTH), pair, z_index)
    share = code_grads.shape[1] // 2
    kept = lax.dynamic_slice_in_dim(code_grads, tensor * share, share, 1)
    sent = lax.dynamic_slice_in_dim(code_grads, (1 - tensor) * share, share, 1).astype(bf16)

    def code_exchange(others):
        (late,) = couple((sent,), others)
        return lax.ppermute(late, "tensor", [(0, 1), (1, 0)])

    summed, got = reduce_weights(*held, corners, code_exchange)
    got = got.astype(f32)
    code_out = jnp.where(
        tensor == 0, jnp.concatenate([kept, got], axis=0), jnp.concatenate([got, kept], axis=0)
    )

    mine = lax.dynamic_index_in_dim(summed, core, 0, keepdims=False)
    other = core_swap(lax.dynamic_index_in_dim(summed, 1 - core, 0, keepdims=False))
    full = jnp.where(
        core == 0,
        jnp.concatenate([mine, other], axis=-1),
        jnp.concatenate([other, mine], axis=-1),
    )
    return (code_out[None], full[0][None], full[1][None])


def solution(mesh):
    in_specs = (
        P(None, "dp", None),
        P(None, "dp"),
        P("pipe", "dp", "tensor"),
        P("pipe", "dp", "tensor"),
        P(),
    )
    out_specs = (
        P("pipe", None, ("dp", "tensor"), None),
        P("pipe", "dp", "tensor"),
        P("pipe", "dp", "tensor"),
    )
    return jax.shard_map(
        on_device, mesh=mesh, in_specs=in_specs, out_specs=out_specs, check_vma=False
    )
```

```python
import functools

import jax
import jax.numpy as jnp
from jax import lax
from jax.experimental import pallas as pl
from jax.experimental.pallas import tpu as pltpu
from jax.sharding import PartitionSpec as P

eps = 1e-05
loss_scale = 512.0
f32 = jnp.float32
bf16 = jnp.bfloat16

Z = 8
SUB = 32
WIDTH = 512
SPAN = 2048
COLS = 4096
XPART = 896
ZPART = SPAN - XPART
TILE = 1024
NEAR = (0, 1, 2, 6, 7)
FAR = (3, 4, 5)
MIB = 1024 * 1024
MICROS = 2
STAGES = 4


def core_swap(value):
    return lax.ppermute(value, "pipe", [(i, i ^ 1) for i in range(8)])


def y_shift(value, steps):
    return lax.ppermute(
        value, "pipe", [(i, i + 2 * steps) for i in range(8) if 0 <= i + 2 * steps < 8]
    )


def z_shift(value, steps):
    return lax.ppermute(
        value, "dp", [(x * Z + z, x * Z + (z + steps) % Z) for x in range(2) for z in range(Z)]
    )


def swap_a(value):
    return lax.ppermute(value, "dp", [(x * Z + z, (1 - x) * Z + z) for x in range(2) for z in range(Z)])


def swap_b(value):
    pairs = [
        ((x * Z + z) * 2 + t, ((1 - x) * Z + z) * 2 + 1 - t)
        for x in range(2)
        for z in range(Z)
        for t in range(2)
    ]
    return lax.ppermute(value, ("dp", "tensor"), pairs)


def swap_far(value):
    return lax.ppermute(value, "tensor", [(0, 1), (1, 0)])


def fenced(*values):
    return lax.optimization_barrier(values)


def copy_kernel(moves, n_in, *refs):
    z_ref, sources = refs[0], refs[1 : n_in + 1]
    targets, sems = refs[n_in + 1 : n_in + 3], refs[n_in + 3]
    copies = []
    for k, (which, src, section, dst) in enumerate(moves):
        rows, columns = dst
        if isinstance(rows, tuple):
            start, z = rows
            start = pl.multiple_of(start + lax.rem(z - z_ref[0] + Z, Z) * SUB, SUB)
            rows = pl.ds(start, SUB)
        copy = pltpu.make_async_copy(
            sources[which].at[src], targets[section].at[:, rows, columns], sems.at[k]
        )
        copy.start()
        copies.append(copy)
    for copy in copies:
        copy.wait()


def place(z_index, pieces, moves):
    vmem, hbm = pl.BlockSpec(memory_space=pltpu.VMEM), pl.BlockSpec(memory_space=pl.ANY)
    return pl.pallas_call(
        functools.partial(copy_kernel, moves, len(pieces)),
        out_shape=[jax.ShapeDtypeStruct((2, WIDTH, COLS), bf16)] * 2,
        in_specs=[pl.BlockSpec(memory_space=pltpu.SMEM)] + [hbm] * len(pieces),
        out_specs=[vmem, vmem],
        scratch_shapes=[pltpu.SemaphoreType.DMA((len(moves),))],
        compiler_params=pltpu.CompilerParams(vmem_limit_bytes=18 * MIB),
    )(z_index, *pieces)


def spot(xr, dz, tr, low, high):
    row = (xr * Z + dz) * SUB
    return (slice(row, row + SUB), slice(tr * SPAN + low, tr * SPAN + high))


def narrow_moves(group, blocks, pieces, moves):
    for section in range(2):
        for (tr, xr), block in zip(((0, 0), (0, 1), (1, 1), (1, 0)), blocks[section]):
            for k, dz in enumerate(group):
                moves.append((len(pieces), (k,), section, spot(xr, dz, tr, XPART, SPAN)))
            pieces.append(block)


def ring_moves(gathered, pieces, moves):
    for section in range(2):
        for z in range(Z):
            for tr in range(2):
                for xr in range(2):
                    columns = slice(tr * SPAN, tr * SPAN + XPART)
                    moves.append(
                        (len(pieces), (z, tr, xr, section), section, ((xr * Z * SUB, z), columns))
                    )
    pieces.append(gathered)


Z_GROUPS = [list(range(Z)), list(range(Z, 2 * Z))]


def gather_weights(dec_weight, enc_weight, core, z_index):
    own = jnp.stack([dec_weight[0], enc_weight[0]])
    mine = lax.dynamic_slice_in_dim(own, core * SPAN, SPAN, 2)
    other = core_swap(lax.dynamic_slice_in_dim(own, (1 - core) * SPAN, SPAN, 2))
    first = core == 0
    block = jnp.stack([jnp.where(first, mine, other), jnp.where(first, other, mine)])
    part_x, part_z = block[..., :XPART], block[..., XPART:]

    a, b, d, u1, d1 = fenced(
        swap_a(part_x),
        swap_b(part_x),
        swap_far(part_x),
        z_shift(part_z, 1),
        z_shift(part_z, -1),
    )
    ring = jnp.stack([jnp.stack([part_x, a]), jnp.stack([d, b])])
    gathered = lax.all_gather(ring, "dp", axis=0, axis_index_groups=Z_GROUPS)
    u2, d2 = fenced(z_shift(u1, 1), z_shift(d1, -1))
    near = [jnp.stack([t[s] for t in (part_z, d1, d2, u2, u1)]) for s in range(2)]
    near_a1, near_b0, u3, d3, near_a0, near_b1 = fenced(
        swap_a(near[1]),
        swap_b(near[0]),
        z_shift(u2, 1),
        z_shift(d2, -1),
        swap_a(near[0]),
        swap_b(near[1]),
    )
    near_d0, near_d1, u4, d4 = fenced(
        swap_a(near_b0), swap_b(near_a1), z_shift(u3[:1], 1), z_shift(d3[1:], -1)
    )
    far = [jnp.stack([d3[0], u4[0], u3[0]]), jnp.stack([d3[1], d4[0], u3[1]])]
    far_a1, far_b0, far_a0, far_b1 = fenced(
        swap_a(far[1]), swap_b(far[0]), swap_a(far[0]), swap_b(far[1])
    )
    far_d0, far_d1 = swap_a(far_b0), swap_b(far_a1)

    pieces, moves = [], []
    narrow_moves(
        NEAR,
        ((near[0], near_a0, near_b0, near_d0), (near[1], near_a1, near_b1, near_d1)),
        pieces,
        moves,
    )
    narrow_moves(
        FAR,
        ((far[0], far_a0, far_b0, far_d0), (far[1], far_a1, far_b1, far_d1)),
        pieces,
        moves,
    )
    ring_moves(gathered, pieces, moves)
    return place(z_index, pieces, moves)


def add(*terms):
    return functools.reduce(lambda a, b: a + b, [t.astype(f32) for t in terms])


def add_low(whole, part, axis):
    low, high = jnp.split(whole, 2, axis)
    return jnp.concatenate([add(low, part).astype(bf16), high], axis=axis)


def add_high(whole, part, axis):
    low, high = jnp.split(whole, 2, axis)
    return jnp.concatenate([low, add(high, part).astype(bf16)], axis=axis)


def couple(results, others):
    return lax.optimization_barrier((tuple(results), tuple(others)))[0]


def reduce_weights(ring, near, far, corners, code_exchange):
    (near_0, far_0), (near_1, far_1) = corners
    ring_sum = lax.psum_scatter(
        ring, "dp", scatter_dimension=0, axis_index_groups=Z_GROUPS, tiled=True
    )[0]
    x_res = (swap_a(far_0[0]), swap_b(far_1[0]))
    x_send = (
        add_high(far[0, 1], x_res[1][:, None], 1),
        add_low(far[1, 1], x_res[0][:, None], 1),
    )
    x_res = (swap_a(x_send[0]), swap_b(x_send[1]))
    far_sum = add(far[0, 0], *x_res).astype(bf16)
    x_send = couple((near_0[0], near_1[0]), (far_sum,))
    n_res = (z_shift(far_sum[1, :1], 1), z_shift(far_sum[1, 1:], -1))
    x_res = (swap_a(x_send[0]), swap_b(x_send[1]))
    n_send = (add_low(far_sum[0], n_res[0], 0), add_high(far_sum[2], n_res[1], 0))
    x_res = couple(x_res, n_send)
    x_send = (
        add_high(near[0, 1], x_res[1][:, None], 1),
        add_low(near[1, 1], x_res[0][:, None], 1),
    )
    n_res = couple((z_shift(n_send[0], 1), z_shift(n_send[1], -1)), x_send)
    x_res = (swap_a(x_send[0]), swap_b(x_send[1]))
    near_sum = add(near[0, 0], *x_res).astype(bf16)
    n_send = (add(near_sum[2], n_res[0]).astype(bf16), add(near_sum[3], n_res[1]).astype(bf16))
    got = code_exchange(n_send)
    n_res = (z_shift(n_send[0], 1), z_shift(n_send[1], -1))
    (ring_sum,) = couple((ring_sum,), (near_sum,))
    x_res = (swap_a(ring_sum[0, 1]), swap_b(ring_sum[1, 1]), swap_far(ring_sum[1, 0]))
    n_send = (add(near_sum[1], n_res[0]).astype(bf16), add(near_sum[4], n_res[1]).astype(bf16))
    n_send = couple(n_send, (got,))
    n_res = (z_shift(n_send[0], 1), z_shift(n_send[1], -1))
    return (
        jnp.concatenate([add(ring_sum[0, 0], *x_res), add(near_sum[0], *n_res)], axis=-1),
        got,
    )


def norm_of(codes):
    values = codes.astype(f32)
    scales = lax.rsqrt(jnp.mean(values * values, axis=-1, keepdims=True) + eps)
    return values, scales


def grad_through_norm(grad_out, codes, left, right):
    values, scales = norm_of(codes)
    summed = left.astype(f32) + right.astype(f32)
    inner = jnp.mean(summed * values, axis=-1, keepdims=True)
    return (
        grad_out.astype(f32) + scales * summed - values * (scales * scales * scales) * inner
    )


def dot_rows(left, right):
    return lax.dot_general(left, right, (((1,), (0,)), ((), ())), preferred_element_type=f32)


def dot_last(left, right):
    return lax.dot_general(left, right, (((1,), (1,)), ((), ())), preferred_element_type=f32)


def dot_first(left, right):
    return lax.dot_general(left, right, (((0,), (0,)), ((), ())), preferred_element_type=f32)


def forward_kernel(n_terms, keep, *refs):
    terms, weight_ref, outs = refs[:n_terms], refs[n_terms], refs[n_terms + 1 :]
    code_ref, part_ref = outs[:2]
    codes = terms[1][...].astype(f32)
    if n_terms == 3:
        codes = codes + terms[2][...].astype(f32)
    codes = (terms[0][...].astype(f32) + codes).astype(bf16)
    code_ref[...] = codes
    values, scales = norm_of(codes)
    normed = (values * scales).astype(bf16)
    total = None
    for low in range(0, COLS, TILE):
        span = slice(low, low + TILE)
        half = 0.5 * dot_rows(normed, weight_ref[0, :, span])
        bend = jnp.tanh(half)
        gated = (half + half * bend).astype(bf16)
        if keep:
            outs[2][:, span] = gated
            outs[3][:, span] = ((0.5 + 0.5 * bend) * (1.0 + half * (1.0 - bend))).astype(bf16)
        part = dot_last(gated, weight_ref[1, :, span])
        total = part if total is None else total + part
    part_ref[...] = total.astype(bf16)


def section_cost(rows):
    return pl.CostEstimate(
        flops=4 * rows * WIDTH * COLS,
        bytes_accessed=4 * WIDTH * COLS + 8 * rows * WIDTH,
        transcendentals=rows * COLS,
    )


def section_forward(terms, weights, keep):
    rows = terms[0].shape[0]
    out_shape = [jax.ShapeDtypeStruct((rows, WIDTH), bf16)] * 2
    if keep:
        out_shape += [jax.ShapeDtypeStruct((rows, COLS), bf16)] * 2
    return pl.pallas_call(
        functools.partial(forward_kernel, len(terms), keep),
        out_shape=out_shape,
        compiler_params=pltpu.CompilerParams(vmem_limit_bytes=16 * MIB),
        cost_estimate=section_cost(rows),
    )(*terms, weights)


def backward_kernel(n_terms, keep, *refs):
    terms, slope_ref, weight_ref = refs[:n_terms], refs[n_terms], refs[n_terms + 1]
    outs = refs[n_terms + 2 :]
    grad_ref, part_ref = outs[:2]
    if n_terms == 2:
        grad = terms[0][...].astype(f32) + terms[1][...].astype(f32)
    else:
        grad = grad_through_norm(*[t[...] for t in terms])
        if keep:
            outs[3][...] = grad
    grad = grad.astype(bf16)
    grad_ref[...] = grad
    total = None
    for low in range(0, COLS, TILE):
        span = slice(low, low + TILE)
        gated_grad = dot_rows(grad, weight_ref[1, :, span])
        hidden_grad = (gated_grad * slope_ref[:, span].astype(f32)).astype(bf16)
        if keep:
            outs[2][:, span] = hidden_grad
        part = dot_last(hidden_grad, weight_ref[0, :, span])
        total = part if total is None else total + part
    part_ref[...] = total.astype(bf16)


def section_backward(terms, slope, weights, keep):
    rows = terms[0].shape[0]
    out_shape = [jax.ShapeDtypeStruct((rows, WIDTH), bf16)] * 2
    if keep:
        out_shape += [jax.ShapeDtypeStruct((rows, COLS), bf16)]
        if len(terms) > 2:
            out_shape += [jax.ShapeDtypeStruct((rows, WIDTH), f32)]
    return pl.pallas_call(
        functools.partial(backward_kernel, len(terms), keep),
        out_shape=out_shape,
        compiler_params=pltpu.CompilerParams(vmem_limit_bytes=16 * MIB),
        cost_estimate=section_cost(rows),
    )(*terms, slope, weights)


def norm_grad_kernel(grad_ref, code_ref, left_ref, right_ref, out_ref):
    out_ref[...] = grad_through_norm(
        grad_ref[...], code_ref[...], left_ref[...], right_ref[...]
    ).astype(out_ref.dtype)


def norm_grad(grad, codes, left, right, dtype):
    return pl.pallas_call(
        norm_grad_kernel,
        out_shape=jax.ShapeDtypeStruct(grad.shape, dtype),
        compiler_params=pltpu.CompilerParams(vmem_limit_bytes=8 * MIB),
    )(grad, codes, left, right)


def seed_kernel(flag_ref, lengths_ref, code_ref, left_ref, right_ref, head_ref, out_ref):
    codes = (
        code_ref[...].astype(f32) + (left_ref[...].astype(f32) + right_ref[...].astype(f32))
    ).astype(bf16)
    head = head_ref[...].astype(f32)
    all_scores = jnp.sum(codes.astype(f32) * head, axis=-1, keepdims=True)
    flag = jnp.full((1, 1), flag_ref[0], jnp.int32).astype(f32)
    rows = all_scores.shape[0] // MICROS
    seq_len = rows // 2
    for micro in range(MICROS):
        scores = all_scores[micro * rows : (micro + 1) * rows]
        position = lax.broadcasted_iota(jnp.int32, (rows, 1), 0)
        chosen_length, other_length = lengths_ref[micro, 0], lengths_ref[micro, 1]
        chosen = jnp.where(position < seq_len, 1.0, 0.0)
        limit = jnp.where(position < seq_len, chosen_length, other_length + seq_len)
        valid = jnp.where(position < limit, 1.0, 0.0)
        chosen_count = jnp.full((1, 1), chosen_length, jnp.int32).astype(f32)
        other_count = jnp.full((1, 1), other_length, jnp.int32).astype(f32)
        chosen_sum = jnp.sum(scores * valid * chosen, axis=0, keepdims=True)
        other_sum = jnp.sum(scores * valid * (1.0 - chosen), axis=0, keepdims=True)
        gap = other_sum / other_count - chosen_sum / chosen_count
        weight = loss_scale * jax.nn.sigmoid(gap)
        token = (1.0 - chosen) * (weight / other_count) - chosen * (weight / chosen_count)
        token = token * valid * flag
        out_ref[micro * rows : (micro + 1) * rows, :] = (token * head).astype(bf16)


def reward_seed(flag, lengths, codes, left, right, head):
    vmem = pl.BlockSpec(memory_space=pltpu.VMEM)
    smem = pl.BlockSpec(memory_space=pltpu.SMEM)
    return pl.pallas_call(
        seed_kernel,
        in_specs=[smem, smem, vmem, vmem, vmem, vmem],
        out_specs=vmem,
        out_shape=jax.ShapeDtypeStruct(codes.shape, bf16),
        compiler_params=pltpu.CompilerParams(vmem_limit_bytes=8 * MIB),
    )(flag, lengths, codes, left, right, head)


def weight_grad_kernel(*refs):
    z_ref, ins = refs[0], refs[1:9]
    ring_ref, near_ref, far_ref = refs[9:12]
    corners = refs[12:]

    def section_body(section):
        grad_ref, code_ref, gated_ref, hidden_ref = ins[4 * section : 4 * section + 4]
        near_corner, far_corner = corners[2 * section : 2 * section + 2]
        values, scales = norm_of(code_ref[...])
        normed = (values * scales).astype(bf16)
        for mat, (left, right) in enumerate(((normed, hidden_ref), (grad_ref[...], gated_ref))):
            for low, high in ((0, XPART), (XPART, SPAN)):
                result = dot_first(left, right[:, low:high]).astype(bf16)
                for xr in range(2):
                    for dz in range(Z):
                        row = (xr * Z + dz) * SUB
                        piece = result[row : row + SUB]
                        if low == 0:
                            ring_ref[lax.rem(z_ref[0] + dz, Z), 0, xr, 0, mat] = piece
                        elif dz in NEAR:
                            k = NEAR.index(dz)
                            near_ref[0, xr, k, 0, mat] = piece
                            if xr == 0:
                                near_corner[0, k, mat] = piece
                        else:
                            k = FAR.index(dz)
                            far_ref[0, xr, k, 0, mat] = piece
                            if xr == 0:
                                far_corner[0, k, mat] = piece

    for section in range(2):
        pl.when(pl.program_id(0) == section)(functools.partial(section_body, section))


def weight_grads(z_index, grads, codes, gated, hidden):
    rows = grads[0].shape[0]
    narrow = pl.BlockSpec((rows, WIDTH), lambda s, t: (0, 0))
    wide = pl.BlockSpec((rows, SPAN), lambda s, t: (0, t))

    def group_spec(count):
        return pl.BlockSpec((1, 2, count, 1, 2, SUB, ZPART), lambda s, t: (t, 0, 0, s, 0, 0, 0))

    def corner_spec(count):
        return pl.BlockSpec((1, count, 2, SUB, ZPART), lambda s, t: (0, 0, 0, 0, 0))

    def corner_shape(count):
        return jax.ShapeDtypeStruct((1, count, 2, SUB, ZPART), bf16)

    ins = []
    for section in range(2):
        ins += [grads[section], codes[section], gated[section], hidden[section]]
    made = pl.pallas_call(
        weight_grad_kernel,
        grid=(2, 2),
        in_specs=[pl.BlockSpec(memory_space=pltpu.SMEM)] + [narrow, narrow, wide, wide] * 2,
        out_specs=[
            pl.BlockSpec((Z, 1, 2, 1, 2, SUB, XPART), lambda s, t: (0, t, 0, s, 0, 0, 0)),
            group_spec(len(NEAR)),
            group_spec(len(FAR)),
        ]
        + [corner_spec(len(NEAR)), corner_spec(len(FAR))] * 2,
        out_shape=[
            jax.ShapeDtypeStruct((Z, 2, 2, 2, 2, SUB, XPART), bf16),
            jax.ShapeDtypeStruct((2, 2, len(NEAR), 2, 2, SUB, ZPART), bf16),
            jax.ShapeDtypeStruct((2, 2, len(FAR), 2, 2, SUB, ZPART), bf16),
        ]
        + [corner_shape(len(NEAR)), corner_shape(len(FAR))] * 2,
        compiler_params=pltpu.CompilerParams(vmem_limit_bytes=36 * MIB),
        cost_estimate=pl.CostEstimate(
            flops=8 * rows * WIDTH * COLS,
            bytes_accessed=8 * WIDTH * COLS,
            transcendentals=0,
        ),
    )(z_index, *ins)
    return made[:3], (made[3:5], made[5:7])


def to_local(value, pair, z_index):
    lead = value.shape[:-1]
    value = value.reshape(lead + (2, Z, SUB))
    axis = len(lead)
    value = jnp.where(pair == 0, value, jnp.flip(value, axis))
    doubled = jnp.concatenate([value, value], axis=axis + 1)
    return lax.dynamic_slice_in_dim(doubled, z_index, Z, axis + 1).reshape(lead + (WIDTH,))


def to_global(value, pair, z_index):
    return to_local(value, pair, (Z - z_index) % Z)


def on_device(codes_in, lengths, dec_weight, enc_weight, head):
    pipe = lax.axis_index("pipe")
    core, stage = pipe % 2, pipe // 2
    tensor = lax.axis_index("tensor")
    dp = lax.axis_index("dp")
    pair, z_index = dp // Z, dp % Z

    weights = gather_weights(dec_weight, enc_weight, core, z_index[None])

    codes_in = lax.dynamic_slice_in_dim(codes_in, tensor * MICROS, MICROS, 0)
    lengths = lax.dynamic_slice_in_dim(lengths, tensor * MICROS, MICROS, 0)
    codes_in = to_local(codes_in, pair, z_index)
    codes_in = jnp.where(stage == 0, codes_in, jnp.zeros_like(codes_in))
    head = to_local(head[None], pair, z_index)
    is_last = (stage == STAGES - 1).astype(jnp.int32)[None]

    codes_in = codes_in.reshape(-1, WIDTH)
    blank = jnp.zeros_like(codes_in)
    received = blank
    for step in range(STAGES):
        keep = step == STAGES - 1
        first = section_forward([received, codes_in], weights[0], keep)
        second = section_forward([first[0], first[1], core_swap(first[1])], weights[1], keep)
        across = core_swap(second[1])
        if not keep:
            received = y_shift(add(second[0], add(second[1], across)).astype(bf16), 1)
    codes, gated, slope = (first[0], second[0]), (first[2], second[2]), (first[3], second[3])
    seed = reward_seed(is_last, lengths, second[0], second[1], across, head)

    received = blank
    for step in range(STAGES):
        keep = step == STAGES - 1
        second = section_backward([received, seed], slope[1], weights[1], keep)
        second_across = core_swap(second[1])
        first = section_backward(
            [second[0], codes[1], second[1], second_across], slope[0], weights[0], keep
        )
        first_across = core_swap(first[1])
        passed = norm_grad(first[0], codes[0], first[1], first_across, f32 if keep else bf16)
        if not keep:
            received = y_shift(passed, -1)

    held, corners = weight_grads(
        z_index[None],
        (first[0], second[0]),
        codes,
        gated,
        (first[2], second[2]),
    )

    code_grads = jnp.where(core == 0, passed, first[3])
    code_grads = to_global(code_grads.reshape(MICROS, -1, WIDTH), pair, z_index)
    share = code_grads.shape[1] // 2
    kept = lax.dynamic_slice_in_dim(code_grads, tensor * share, share, 1)
    sent = lax.dynamic_slice_in_dim(code_grads, (1 - tensor) * share, share, 1).astype(bf16)

    def code_exchange(others):
        (late,) = couple((sent,), others)
        return swap_far(late)

    summed, got = reduce_weights(*held, corners, code_exchange)
    got = got.astype(f32)
    code_out = jnp.where(
        tensor == 0, jnp.concatenate([kept, got], axis=0), jnp.concatenate([got, kept], axis=0)
    )

    mine = lax.dynamic_index_in_dim(summed, core, 0, keepdims=False)
    other = core_swap(lax.dynamic_index_in_dim(summed, 1 - core, 0, keepdims=False))
    full = jnp.where(
        core == 0,
        jnp.concatenate([mine, other], axis=-1),
        jnp.concatenate([other, mine], axis=-1),
    )
    return (code_out[None], full[0][None], full[1][None])


def solution(mesh):
    in_specs = (
        P(None, "dp", None),
        P(None, "dp"),
        P("pipe", "dp", "tensor"),
        P("pipe", "dp", "tensor"),
        P(),
    )
    out_specs = (
        P("pipe", None, ("dp", "tensor"), None),
        P("pipe", "dp", "tensor"),
        P("pipe", "dp", "tensor"),
    )
    return jax.shard_map(
        on_device, mesh=mesh, in_specs=in_specs, out_specs=out_specs, check_vma=False
    )
```

```python
import functools

import jax
import jax.numpy as jnp
from jax import lax
from jax.experimental import pallas as pl
from jax.experimental.pallas import tpu as pltpu
from jax.sharding import PartitionSpec as P

eps = 1e-05
loss_scale = 512.0
f32 = jnp.float32
bf16 = jnp.bfloat16

Z = 8
SUB = 32
WIDTH = 512
SPAN = 2048
COLS = 4096
XPART = 896
ZPART = SPAN - XPART
XSUM = 1024
ZSUM = SPAN - XSUM
TILE = 1024
NEAR = (0, 1, 2, 6, 7)
FAR = (3, 4, 5)
MIB = 1024 * 1024
MICROS = 2
STAGES = 4


def core_swap(value):
    return lax.ppermute(value, "pipe", [(i, i ^ 1) for i in range(8)])


def y_shift(value, steps):
    return lax.ppermute(
        value, "pipe", [(i, i + 2 * steps) for i in range(8) if 0 <= i + 2 * steps < 8]
    )


def z_shift(value, steps):
    return lax.ppermute(
        value, "dp", [(x * Z + z, x * Z + (z + steps) % Z) for x in range(2) for z in range(Z)]
    )


def swap_a(value):
    return lax.ppermute(value, "dp", [(x * Z + z, (1 - x) * Z + z) for x in range(2) for z in range(Z)])


def swap_b(value):
    pairs = [
        ((x * Z + z) * 2 + t, ((1 - x) * Z + z) * 2 + 1 - t)
        for x in range(2)
        for z in range(Z)
        for t in range(2)
    ]
    return lax.ppermute(value, ("dp", "tensor"), pairs)


def swap_far(value):
    return lax.ppermute(value, "tensor", [(0, 1), (1, 0)])


def fenced(*values):
    return lax.optimization_barrier(values)


def copy_kernel(moves, n_in, *refs):
    z_ref, sources = refs[0], refs[1 : n_in + 1]
    targets, sems = refs[n_in + 1 : n_in + 3], refs[n_in + 3]
    copies = []
    for k, (which, src, section, dst) in enumerate(moves):
        rows, columns = dst
        if isinstance(rows, tuple):
            start, z = rows
            start = pl.multiple_of(start + lax.rem(z - z_ref[0] + Z, Z) * SUB, SUB)
            rows = pl.ds(start, SUB)
        copy = pltpu.make_async_copy(
            sources[which].at[src], targets[section].at[:, rows, columns], sems.at[k]
        )
        copy.start()
        copies.append(copy)
    for copy in copies:
        copy.wait()


def place(z_index, pieces, moves):
    vmem, hbm = pl.BlockSpec(memory_space=pltpu.VMEM), pl.BlockSpec(memory_space=pl.ANY)
    return pl.pallas_call(
        functools.partial(copy_kernel, moves, len(pieces)),
        out_shape=[jax.ShapeDtypeStruct((2, WIDTH, COLS), bf16)] * 2,
        in_specs=[pl.BlockSpec(memory_space=pltpu.SMEM)] + [hbm] * len(pieces),
        out_specs=[vmem, vmem],
        scratch_shapes=[pltpu.SemaphoreType.DMA((len(moves),))],
        compiler_params=pltpu.CompilerParams(vmem_limit_bytes=18 * MIB),
    )(z_index, *pieces)


def spot(xr, dz, tr, low, high):
    row = (xr * Z + dz) * SUB
    return (slice(row, row + SUB), slice(tr * SPAN + low, tr * SPAN + high))


def narrow_moves(group, blocks, pieces, moves):
    for section in range(2):
        for (tr, xr), block in zip(((0, 0), (0, 1), (1, 1), (1, 0)), blocks[section]):
            for k, dz in enumerate(group):
                moves.append((len(pieces), (k,), section, spot(xr, dz, tr, XPART, SPAN)))
            pieces.append(block)


def ring_moves(gathered, pieces, moves):
    for section in range(2):
        for z in range(Z):
            for tr in range(2):
                for xr in range(2):
                    columns = slice(tr * SPAN, tr * SPAN + XPART)
                    moves.append(
                        (len(pieces), (z, tr, xr, section), section, ((xr * Z * SUB, z), columns))
                    )
    pieces.append(gathered)


Z_GROUPS = [list(range(Z)), list(range(Z, 2 * Z))]


def gather_weights(dec_weight, enc_weight, core, z_index):
    own = jnp.stack([dec_weight[0], enc_weight[0]])
    mine = lax.dynamic_slice_in_dim(own, core * SPAN, SPAN, 2)
    other = core_swap(lax.dynamic_slice_in_dim(own, (1 - core) * SPAN, SPAN, 2))
    first = core == 0
    block = jnp.stack([jnp.where(first, mine, other), jnp.where(first, other, mine)])
    part_x, part_z = block[..., :XPART], block[..., XPART:]

    u1, d1 = z_shift(part_z, 1), z_shift(part_z, -1)
    a, b, d = fenced(swap_a(part_x), swap_b(part_x), swap_far(part_x))
    ring = jnp.stack([jnp.stack([part_x, a]), jnp.stack([d, b])])
    gathered = lax.all_gather(ring, "dp", axis=0, axis_index_groups=Z_GROUPS)
    u2, d2 = fenced(z_shift(u1, 1), z_shift(d1, -1))
    near = [jnp.stack([t[s] for t in (part_z, d1, d2, u2, u1)]) for s in range(2)]
    near_a1, near_b0, u3, d3, near_a0, near_b1 = fenced(
        swap_a(near[1]),
        swap_b(near[0]),
        z_shift(u2, 1),
        z_shift(d2, -1),
        swap_a(near[0]),
        swap_b(near[1]),
    )
    near_d0, near_d1, u4, d4 = fenced(
        swap_a(near_b0), swap_b(near_a1), z_shift(u3[:1], 1), z_shift(d3[1:], -1)
    )
    far = [jnp.stack([d3[0], u4[0], u3[0]]), jnp.stack([d3[1], d4[0], u3[1]])]
    far_a1, far_b0, far_a0, far_b1 = fenced(
        swap_a(far[1]), swap_b(far[0]), swap_a(far[0]), swap_b(far[1])
    )
    far_d0, far_d1 = swap_a(far_b0), swap_b(far_a1)

    pieces, moves = [], []
    narrow_moves(
        NEAR,
        ((near[0], near_a0, near_b0, near_d0), (near[1], near_a1, near_b1, near_d1)),
        pieces,
        moves,
    )
    narrow_moves(
        FAR,
        ((far[0], far_a0, far_b0, far_d0), (far[1], far_a1, far_b1, far_d1)),
        pieces,
        moves,
    )
    ring_moves(gathered, pieces, moves)
    return place(z_index, pieces, moves)


def add(*terms):
    return functools.reduce(lambda a, b: a + b, [t.astype(f32) for t in terms])


def add_low(whole, part, axis):
    low, high = jnp.split(whole, 2, axis)
    return jnp.concatenate([add(low, part).astype(bf16), high], axis=axis)


def add_high(whole, part, axis):
    low, high = jnp.split(whole, 2, axis)
    return jnp.concatenate([low, add(high, part).astype(bf16)], axis=axis)


def couple(results, others):
    return lax.optimization_barrier((tuple(results), tuple(others)))[0]


def reduce_weights(ring, near, far, corners, code_exchange):
    (near_0, far_0), (near_1, far_1) = corners
    ring_sum = lax.psum_scatter(
        ring, "dp", scatter_dimension=0, axis_index_groups=Z_GROUPS, tiled=True
    )[0]
    x_res = (swap_a(far_0[0]), swap_b(far_1[0]))
    x_send = (
        add_high(far[0, 1], x_res[1][:, None], 1),
        add_low(far[1, 1], x_res[0][:, None], 1),
    )
    x_res = (swap_a(x_send[0]), swap_b(x_send[1]))
    far_sum = add(far[0, 0], *x_res).astype(bf16)
    x_send = couple((near_0[0], near_1[0]), (far_sum,))
    n_res = (z_shift(far_sum[1, :1], 1), z_shift(far_sum[1, 1:], -1))
    x_res = (swap_a(x_send[0]), swap_b(x_send[1]))
    n_send = (add_low(far_sum[0], n_res[0], 0), add_high(far_sum[2], n_res[1], 0))
    x_res = couple(x_res, n_send)
    x_send = (
        add_high(near[0, 1], x_res[1][:, None], 1),
        add_low(near[1, 1], x_res[0][:, None], 1),
    )
    n_res = couple((z_shift(n_send[0], 1), z_shift(n_send[1], -1)), x_send)
    x_res = (swap_a(x_send[0]), swap_b(x_send[1]))
    near_sum = add(near[0, 0], *x_res).astype(bf16)
    n_send = (add(near_sum[2], n_res[0]).astype(bf16), add(near_sum[3], n_res[1]).astype(bf16))
    got = code_exchange(n_send)
    n_res = (z_shift(n_send[0], 1), z_shift(n_send[1], -1))
    (ring_sum,) = couple((ring_sum,), (near_sum,))
    x_res = (swap_a(ring_sum[0, 1]), swap_b(ring_sum[1, 1]), swap_far(ring_sum[1, 0]))
    n_send = (add(near_sum[1], n_res[0]).astype(bf16), add(near_sum[4], n_res[1]).astype(bf16))
    n_send = couple(n_send, (got,))
    n_res = (z_shift(n_send[0], 1), z_shift(n_send[1], -1))
    return (
        jnp.concatenate([add(ring_sum[0, 0], *x_res), add(near_sum[0], *n_res)], axis=-1),
        got,
    )


def norm_of(codes):
    values = codes.astype(f32)
    scales = lax.rsqrt(jnp.mean(values * values, axis=-1, keepdims=True) + eps)
    return values, scales


def grad_through_norm(grad_out, codes, left, right):
    values, scales = norm_of(codes)
    summed = left.astype(f32) + right.astype(f32)
    inner = jnp.mean(summed * values, axis=-1, keepdims=True)
    return (
        grad_out.astype(f32) + scales * summed - values * (scales * scales * scales) * inner
    )


def dot_rows(left, right):
    return lax.dot_general(left, right, (((1,), (0,)), ((), ())), preferred_element_type=f32)


def dot_last(left, right):
    return lax.dot_general(left, right, (((1,), (1,)), ((), ())), preferred_element_type=f32)


def dot_first(left, right):
    return lax.dot_general(left, right, (((0,), (0,)), ((), ())), preferred_element_type=f32)


def forward_kernel(n_terms, keep, *refs):
    terms, weight_ref, outs = refs[:n_terms], refs[n_terms], refs[n_terms + 1 :]
    code_ref, part_ref = outs[:2]
    codes = terms[1][...].astype(f32)
    if n_terms == 3:
        codes = codes + terms[2][...].astype(f32)
    codes = (terms[0][...].astype(f32) + codes).astype(bf16)
    code_ref[...] = codes
    values, scales = norm_of(codes)
    normed = (values * scales).astype(bf16)
    total = None
    for low in range(0, COLS, TILE):
        span = slice(low, low + TILE)
        half = 0.5 * dot_rows(normed, weight_ref[0, :, span])
        bend = jnp.tanh(half)
        gated = (half + half * bend).astype(bf16)
        if keep:
            outs[2][:, span] = gated
            outs[3][:, span] = ((0.5 + 0.5 * bend) * (1.0 + half * (1.0 - bend))).astype(bf16)
        part = dot_last(gated, weight_ref[1, :, span])
        total = part if total is None else total + part
    part_ref[...] = total.astype(bf16)


def section_cost(rows):
    return pl.CostEstimate(
        flops=4 * rows * WIDTH * COLS,
        bytes_accessed=4 * WIDTH * COLS + 8 * rows * WIDTH,
        transcendentals=rows * COLS,
    )


def section_forward(terms, weights, keep):
    rows = terms[0].shape[0]
    out_shape = [jax.ShapeDtypeStruct((rows, WIDTH), bf16)] * 2
    if keep:
        out_shape += [jax.ShapeDtypeStruct((rows, COLS), bf16)] * 2
    return pl.pallas_call(
        functools.partial(forward_kernel, len(terms), keep),
        out_shape=out_shape,
        compiler_params=pltpu.CompilerParams(vmem_limit_bytes=16 * MIB),
        cost_estimate=section_cost(rows),
    )(*terms, weights)


def backward_kernel(n_terms, keep, *refs):
    terms, slope_ref, weight_ref = refs[:n_terms], refs[n_terms], refs[n_terms + 1]
    outs = refs[n_terms + 2 :]
    grad_ref, part_ref = outs[:2]
    if n_terms == 2:
        grad = terms[0][...].astype(f32) + terms[1][...].astype(f32)
    else:
        grad = grad_through_norm(*[t[...] for t in terms])
        if keep:
            outs[3][...] = grad
    grad = grad.astype(bf16)
    grad_ref[...] = grad
    total = None
    for low in range(0, COLS, TILE):
        span = slice(low, low + TILE)
        gated_grad = dot_rows(grad, weight_ref[1, :, span])
        hidden_grad = (gated_grad * slope_ref[:, span].astype(f32)).astype(bf16)
        if keep:
            outs[2][:, span] = hidden_grad
        part = dot_last(hidden_grad, weight_ref[0, :, span])
        total = part if total is None else total + part
    part_ref[...] = total.astype(bf16)


def section_backward(terms, slope, weights, keep):
    rows = terms[0].shape[0]
    out_shape = [jax.ShapeDtypeStruct((rows, WIDTH), bf16)] * 2
    if keep:
        out_shape += [jax.ShapeDtypeStruct((rows, COLS), bf16)]
        if len(terms) > 2:
            out_shape += [jax.ShapeDtypeStruct((rows, WIDTH), f32)]
    return pl.pallas_call(
        functools.partial(backward_kernel, len(terms), keep),
        out_shape=out_shape,
        compiler_params=pltpu.CompilerParams(vmem_limit_bytes=16 * MIB),
        cost_estimate=section_cost(rows),
    )(*terms, slope, weights)


def norm_grad_kernel(grad_ref, code_ref, left_ref, right_ref, out_ref):
    out_ref[...] = grad_through_norm(
        grad_ref[...], code_ref[...], left_ref[...], right_ref[...]
    ).astype(out_ref.dtype)


def norm_grad(grad, codes, left, right, dtype):
    return pl.pallas_call(
        norm_grad_kernel,
        out_shape=jax.ShapeDtypeStruct(grad.shape, dtype),
        compiler_params=pltpu.CompilerParams(vmem_limit_bytes=8 * MIB),
    )(grad, codes, left, right)


def seed_kernel(flag_ref, lengths_ref, code_ref, left_ref, right_ref, head_ref, out_ref):
    codes = (
        code_ref[...].astype(f32) + (left_ref[...].astype(f32) + right_ref[...].astype(f32))
    ).astype(bf16)
    head = head_ref[...].astype(f32)
    all_scores = jnp.sum(codes.astype(f32) * head, axis=-1, keepdims=True)
    flag = jnp.full((1, 1), flag_ref[0], jnp.int32).astype(f32)
    rows = all_scores.shape[0] // MICROS
    seq_len = rows // 2
    for micro in range(MICROS):
        scores = all_scores[micro * rows : (micro + 1) * rows]
        position = lax.broadcasted_iota(jnp.int32, (rows, 1), 0)
        chosen_length, other_length = lengths_ref[micro, 0], lengths_ref[micro, 1]
        chosen = jnp.where(position < seq_len, 1.0, 0.0)
        limit = jnp.where(position < seq_len, chosen_length, other_length + seq_len)
        valid = jnp.where(position < limit, 1.0, 0.0)
        chosen_count = jnp.full((1, 1), chosen_length, jnp.int32).astype(f32)
        other_count = jnp.full((1, 1), other_length, jnp.int32).astype(f32)
        chosen_sum = jnp.sum(scores * valid * chosen, axis=0, keepdims=True)
        other_sum = jnp.sum(scores * valid * (1.0 - chosen), axis=0, keepdims=True)
        gap = other_sum / other_count - chosen_sum / chosen_count
        weight = loss_scale * jax.nn.sigmoid(gap)
        token = (1.0 - chosen) * (weight / other_count) - chosen * (weight / chosen_count)
        token = token * valid * flag
        out_ref[micro * rows : (micro + 1) * rows, :] = (token * head).astype(bf16)


def reward_seed(flag, lengths, codes, left, right, head):
    vmem = pl.BlockSpec(memory_space=pltpu.VMEM)
    smem = pl.BlockSpec(memory_space=pltpu.SMEM)
    return pl.pallas_call(
        seed_kernel,
        in_specs=[smem, smem, vmem, vmem, vmem, vmem],
        out_specs=vmem,
        out_shape=jax.ShapeDtypeStruct(codes.shape, bf16),
        compiler_params=pltpu.CompilerParams(vmem_limit_bytes=8 * MIB),
    )(flag, lengths, codes, left, right, head)


def weight_grad_kernel(*refs):
    z_ref, ins = refs[0], refs[1:9]
    ring_ref, near_ref, far_ref = refs[9:12]
    corners = refs[12:]

    def section_body(section):
        grad_ref, code_ref, gated_ref, hidden_ref = ins[4 * section : 4 * section + 4]
        near_corner, far_corner = corners[2 * section : 2 * section + 2]
        values, scales = norm_of(code_ref[...])
        normed = (values * scales).astype(bf16)
        for mat, (left, right) in enumerate(((normed, hidden_ref), (grad_ref[...], gated_ref))):
            for low, high in ((0, XSUM), (XSUM, SPAN)):
                result = dot_first(left, right[:, low:high]).astype(bf16)
                for xr in range(2):
                    for dz in range(Z):
                        row = (xr * Z + dz) * SUB
                        piece = result[row : row + SUB]
                        if low == 0:
                            ring_ref[lax.rem(z_ref[0] + dz, Z), 0, xr, 0, mat] = piece
                        elif dz in NEAR:
                            k = NEAR.index(dz)
                            near_ref[0, xr, k, 0, mat] = piece
                            if xr == 0:
                                near_corner[0, k, mat] = piece
                        else:
                            k = FAR.index(dz)
                            far_ref[0, xr, k, 0, mat] = piece
                            if xr == 0:
                                far_corner[0, k, mat] = piece

    for section in range(2):
        pl.when(pl.program_id(0) == section)(functools.partial(section_body, section))


def weight_grads(z_index, grads, codes, gated, hidden):
    rows = grads[0].shape[0]
    narrow = pl.BlockSpec((rows, WIDTH), lambda s, t: (0, 0))
    wide = pl.BlockSpec((rows, SPAN), lambda s, t: (0, t))

    def group_spec(count):
        return pl.BlockSpec((1, 2, count, 1, 2, SUB, ZSUM), lambda s, t: (t, 0, 0, s, 0, 0, 0))

    def corner_spec(count):
        return pl.BlockSpec((1, count, 2, SUB, ZSUM), lambda s, t: (0, 0, 0, 0, 0))

    def corner_shape(count):
        return jax.ShapeDtypeStruct((1, count, 2, SUB, ZSUM), bf16)

    ins = []
    for section in range(2):
        ins += [grads[section], codes[section], gated[section], hidden[section]]
    made = pl.pallas_call(
        weight_grad_kernel,
        grid=(2, 2),
        in_specs=[pl.BlockSpec(memory_space=pltpu.SMEM)] + [narrow, narrow, wide, wide] * 2,
        out_specs=[
            pl.BlockSpec((Z, 1, 2, 1, 2, SUB, XSUM), lambda s, t: (0, t, 0, s, 0, 0, 0)),
            group_spec(len(NEAR)),
            group_spec(len(FAR)),
        ]
        + [corner_spec(len(NEAR)), corner_spec(len(FAR))] * 2,
        out_shape=[
            jax.ShapeDtypeStruct((Z, 2, 2, 2, 2, SUB, XSUM), bf16),
            jax.ShapeDtypeStruct((2, 2, len(NEAR), 2, 2, SUB, ZSUM), bf16),
            jax.ShapeDtypeStruct((2, 2, len(FAR), 2, 2, SUB, ZSUM), bf16),
        ]
        + [corner_shape(len(NEAR)), corner_shape(len(FAR))] * 2,
        compiler_params=pltpu.CompilerParams(vmem_limit_bytes=36 * MIB),
        cost_estimate=pl.CostEstimate(
            flops=8 * rows * WIDTH * COLS,
            bytes_accessed=8 * WIDTH * COLS,
            transcendentals=0,
        ),
    )(z_index, *ins)
    return made[:3], (made[3:5], made[5:7])


def to_local(value, pair, z_index):
    lead = value.shape[:-1]
    value = value.reshape(lead + (2, Z, SUB))
    axis = len(lead)
    value = jnp.where(pair == 0, value, jnp.flip(value, axis))
    doubled = jnp.concatenate([value, value], axis=axis + 1)
    return lax.dynamic_slice_in_dim(doubled, z_index, Z, axis + 1).reshape(lead + (WIDTH,))


def to_global(value, pair, z_index):
    return to_local(value, pair, (Z - z_index) % Z)


def on_device(codes_in, lengths, dec_weight, enc_weight, head):
    pipe = lax.axis_index("pipe")
    core, stage = pipe % 2, pipe // 2
    tensor = lax.axis_index("tensor")
    dp = lax.axis_index("dp")
    pair, z_index = dp // Z, dp % Z

    weights = gather_weights(dec_weight, enc_weight, core, z_index[None])

    codes_in = lax.dynamic_slice_in_dim(codes_in, tensor * MICROS, MICROS, 0)
    lengths = lax.dynamic_slice_in_dim(lengths, tensor * MICROS, MICROS, 0)
    codes_in = to_local(codes_in, pair, z_index)
    codes_in = jnp.where(stage == 0, codes_in, jnp.zeros_like(codes_in))
    head = to_local(head[None], pair, z_index)
    is_last = (stage == STAGES - 1).astype(jnp.int32)[None]

    codes_in = codes_in.reshape(-1, WIDTH)
    blank = jnp.zeros_like(codes_in)
    received = blank
    for step in range(STAGES):
        keep = step == STAGES - 1
        first = section_forward([received, codes_in], weights[0], keep)
        second = section_forward([first[0], first[1], core_swap(first[1])], weights[1], keep)
        across = core_swap(second[1])
        if not keep:
            received = y_shift(add(second[0], add(second[1], across)).astype(bf16), 1)
    codes, gated, slope = (first[0], second[0]), (first[2], second[2]), (first[3], second[3])
    seed = reward_seed(is_last, lengths, second[0], second[1], across, head)

    received = blank
    for step in range(STAGES):
        keep = step == STAGES - 1
        second = section_backward([received, seed], slope[1], weights[1], keep)
        second_across = core_swap(second[1])
        first = section_backward(
            [second[0], codes[1], second[1], second_across], slope[0], weights[0], keep
        )
        first_across = core_swap(first[1])
        passed = norm_grad(first[0], codes[0], first[1], first_across, f32 if keep else bf16)
        if not keep:
            received = y_shift(passed, -1)

    held, corners = weight_grads(
        z_index[None],
        (first[0], second[0]),
        codes,
        gated,
        (first[2], second[2]),
    )

    code_grads = jnp.where(core == 0, passed, first[3])
    code_grads = to_global(code_grads.reshape(MICROS, -1, WIDTH), pair, z_index)
    share = code_grads.shape[1] // 2
    kept = lax.dynamic_slice_in_dim(code_grads, tensor * share, share, 1)
    sent = lax.dynamic_slice_in_dim(code_grads, (1 - tensor) * share, share, 1).astype(bf16)

    def code_exchange(others):
        (late,) = couple((sent,), others)
        return swap_far(late)

    summed, got = reduce_weights(*held, corners, code_exchange)
    got = got.astype(f32)
    code_out = jnp.where(
        tensor == 0, jnp.concatenate([kept, got], axis=0), jnp.concatenate([got, kept], axis=0)
    )

    mine = lax.dynamic_index_in_dim(summed, core, 0, keepdims=False)
    other = core_swap(lax.dynamic_index_in_dim(summed, 1 - core, 0, keepdims=False))
    full = jnp.where(
        core == 0,
        jnp.concatenate([mine, other], axis=-1),
        jnp.concatenate([other, mine], axis=-1),
    )
    return (code_out[None], full[0][None], full[1][None])


def solution(mesh):
    in_specs = (
        P(None, "dp", None),
        P(None, "dp"),
        P("pipe", "dp", "tensor"),
        P("pipe", "dp", "tensor"),
        P(),
    )
    out_specs = (
        P("pipe", None, ("dp", "tensor"), None),
        P("pipe", "dp", "tensor"),
        P("pipe", "dp", "tensor"),
    )
    return jax.shard_map(
        on_device, mesh=mesh, in_specs=in_specs, out_specs=out_specs, check_vma=False
    )
```
